256 devices in a mesh: leaf: 8 (over x, core), seg: 32 (over y, z).
Axes of the slice: x: 4, y: 4, z: 8, core: 2. Of those that a mesh axis runs over, the one named last changes fastest.
Arguments:
- hidden_states: bfloat16 [8, 8192, 8192], P('leaf', 'seg'), may hold values from -6 to 6
- queries: bfloat16 [8, 8192, 1024], P('leaf', 'seg'), may hold values from -255 to 255
- key_value_weight: bfloat16 [8192, 256], P('seg'), may hold values from -0.0625 to 0.0625
- attention_grad: bfloat16 [8, 8192, 1024], P('leaf', 'seg'), may hold values from -24 to 24
- parents: int32 [8, 32], P('leaf'), may hold values from 0 to 7, as said below
- owners: int32 [8, 32], P('leaf'), may hold values from 0 to 31, each once within a row
- depths: int32 [8, 32], P('leaf'), may hold values from 0 to 3, as said below
Outputs:
- attention: bfloat16 [8, 8192, 1024], P('leaf', 'seg')
- query_grad: bfloat16 [8, 8192, 1024], P('leaf', 'seg')
- kv_grad: float32 [8192, 256], P('seg')
The draws below stay inside these ranges and needn't reach their ends.
Inputs may be any that keep to these rules, and one draw needn't show every extreme that they name: parents[t, 0] = 0; for s >= 1, parents[t, s] < s and depths[t, parents[t, s]] = depths[t, s] - 1; the segments 0 to 7 are exactly those that are parents of other segments. `depths`: segment 0 is the only segment of level 0; the levels agree with parents.
All inputs are finite; a program needn't handle non-finite values.
Results may differ from the reference program's by a relative error of at most 0.038.
The reference program's roundings to bfloat16 on the way count: a program that leaves them out, or rounds other values in their place, can miss the bound.
Values may be sent and summed in bfloat16 or wider, within the bound.
No kernel may reach another device: no remote copies, remote signals or barrier semaphores. Data moves between devices by JAX's collectives and lax.ppermute only.
A program may use at most 128 MiB of HBM per device.

```python
import math
import jax
import jax.numpy as jnp
import numpy as np
from jax import lax

D = 8192
HEAD = 128
HEADS = 8
SEG_LEN = 256
DEPTH = 4
SEGS = 32
TREES = 8


def tree_draw(key):
    key_inner, key_leaf, key_parent = jax.random.split(key, 3)
    inner = max(DEPTH - 1, SEGS // 4)
    seg_ids = jnp.arange(SEGS, dtype=jnp.int32)
    raw_inner = jax.random.randint(key_inner, (TREES, SEGS), 1, DEPTH - 1)
    raw_leaf = jax.random.randint(key_leaf, (TREES, SEGS), 1, DEPTH)
    inner_levels = jnp.where(seg_ids < DEPTH - 1, seg_ids, raw_inner)
    source = np.clip(np.arange(SEGS) - inner, 0, SEGS - 1)
    forced_levels = inner_levels[:, source] + 1
    levels = jnp.where(seg_ids < inner, inner_levels, jnp.where(seg_ids < 2 * inner, forced_levels, raw_leaf)).astype(jnp.int32)
    scores = jax.random.randint(key_parent, (TREES, SEGS, SEGS), 0, 65536) * SEGS + seg_ids[None, None, :]
    favoured = (seg_ids[:, None] >= inner) & (seg_ids[:, None] < 2 * inner) & (seg_ids[None, :] == seg_ids[:, None] - inner)
    scores = scores + jnp.where(favoured, 4194304, 0)[None]
    allowed = (seg_ids[None, None, :] < seg_ids[None, :, None]) & (seg_ids[None, None, :] < inner) & (levels[:, None, :] == levels[:, :, None] - 1)
    scores = jnp.where(allowed, scores, -1)
    parent_ids = jnp.argmax(scores, axis=-1).astype(jnp.int32)
    return (parent_ids, levels)


def draw_parents(key, part):
    return tree_draw(key)[0]


def draw_depths(key, part):
    return tree_draw(key)[1]


def draw_queries(key, part):
    key = jax.random.fold_in(key, 11)
    key_scale, key_value = jax.random.split(key, 2)
    rows = SEGS * SEG_LEN
    scales = jnp.exp(jax.random.uniform(key_scale, (TREES, rows, HEADS, 1), jnp.float32, math.log(0.5), math.log(5.0)))
    base = jnp.clip(jax.random.normal(key_value, (TREES, rows, HEADS, HEAD), jnp.float32), -4.0, 4.0)
    values = base * scales
    return values.reshape(TREES, rows, HEADS * HEAD).astype(jnp.bfloat16)


def shard_levels(own_key, dims, pieces, least, largest):
    loudness = 1.0
    for axis_at, blocks in pieces:
        draws = jax.random.uniform(jax.random.fold_in(jax.random.fold_in(own_key, 6), axis_at), (blocks,), jnp.float32, least / len(pieces), largest / len(pieces))
        loudness = loudness * jnp.repeat(jnp.exp(draws), dims[axis_at] // blocks).reshape((-1,) + (1,) * (len(dims) - 1 - axis_at))
    return loudness


def normal_values(own_key, shape, spread, reach, cuts=(), kind=jnp.bfloat16):
    gain = shard_levels(own_key, shape, cuts, -0.22, 0.18) if cuts else 1.0
    result = jax.random.normal(own_key, shape, jnp.float32) * spread * gain
    return jnp.minimum(jnp.maximum(result, -reach), reach).astype(kind)


def setup_inputs(seed: int = 0) -> dict:
    key_of = jax.random.split(jax.random.key(seed), 8)
    return {
        "hidden_states": normal_values(key_of[0], (TREES, SEGS * SEG_LEN, D), 1.0, 6.0, ((0, 8), (1, 32))),
        "queries": draw_queries(jax.random.fold_in(key_of[7], 71), 0),
        "key_value_weight": normal_values(key_of[2], (D, 2 * HEAD), D ** -0.5, 0.0625, ((0, 32),)),
        "attention_grad": normal_values(key_of[3], (TREES, SEGS * SEG_LEN, HEADS * HEAD), 4.0, 24.0, ((0, 8), (1, 32))),
        "parents": draw_parents(jax.random.fold_in(key_of[7], 71), 0),
        "owners": jax.vmap(lambda own: jax.random.permutation(own, SEGS))(jax.random.split(key_of[5], TREES)).reshape((TREES, SEGS)).astype(jnp.int32),
        "depths": draw_depths(jax.random.fold_in(key_of[7], 71), 0),
    }


def lookup(table, index):
    ids = jnp.arange(table.shape[0], dtype=jnp.int32)
    return jnp.sum(jnp.where(ids == index, table, 0)).astype(jnp.int32)


def attend(query_rows, pairs, level_ok, grad_rows):
    seg_len = query_rows.shape[0]
    factor = HEAD ** -0.5
    keys = pairs[:, :, :HEAD].reshape(DEPTH * seg_len, HEAD).astype(jnp.float32)
    values = pairs[:, :, HEAD:].reshape(DEPTH * seg_len, HEAD).astype(jnp.float32)
    heads_q = query_rows.reshape(seg_len, HEADS, HEAD).astype(jnp.float32)
    heads_g = grad_rows.reshape(seg_len, HEADS, HEAD).astype(jnp.float32)
    scores = jnp.einsum('ihd,jd->hij', heads_q, keys) * factor
    row_ids = jnp.arange(seg_len, dtype=jnp.int32)[:, None]
    col_ids = jnp.arange(DEPTH * seg_len, dtype=jnp.int32)[None, :]
    slot_ids = col_ids // seg_len
    within = col_ids % seg_len
    allowed = jnp.where(slot_ids == 0, within <= row_ids, level_ok[slot_ids])
    masked = jnp.where(allowed[None], scores, -jnp.inf)
    peak = jnp.max(masked, axis=-1, keepdims=True)
    expd = jnp.exp(masked - peak)
    probs = (expd / jnp.sum(expd, axis=-1, keepdims=True)).astype(jnp.bfloat16)
    probs_f = probs.astype(jnp.float32)
    output = jnp.einsum('hij,jd->ihd', probs_f, values).astype(jnp.bfloat16)
    dprobs = jnp.einsum('ihd,jd->hij', heads_g, values)
    centre = jnp.sum(probs_f * dprobs, axis=-1, keepdims=True)
    dscores = (probs_f * (dprobs - centre)).astype(jnp.bfloat16).astype(jnp.float32)
    query_grad = (jnp.einsum('hij,jd->ihd', dscores, keys) * factor).astype(jnp.bfloat16)
    key_part = jnp.einsum('hij,ihd->jd', dscores, heads_q) * factor
    value_part = jnp.einsum('hij,ihd->jd', probs_f, heads_g)
    slot_grads = jnp.concatenate([key_part, value_part], axis=-1).reshape(DEPTH, seg_len, 2 * HEAD)
    return (output.reshape(seg_len, HEADS * HEAD), query_grad.reshape(seg_len, HEADS * HEAD), slot_grads)


def tree_pass(tokens, query_all, grad_all, parent_row, owner_row, depth_row, weight):
    pairs = jnp.dot(tokens, weight, preferred_element_type=jnp.float32).astype(jnp.bfloat16)
    blocks3 = pairs.reshape(SEGS, SEG_LEN, 2 * HEAD)
    seg_ids = jnp.arange(SEGS, dtype=jnp.int32)

    def one_block(position):
        current = jnp.sum(jnp.where(owner_row == position, seg_ids, 0)).astype(jnp.int32)
        my_depth = lookup(depth_row, current)
        level_ok = jnp.arange(DEPTH, dtype=jnp.int32) <= my_depth
        holders = [position]
        ancestor = current
        for level in range(1, DEPTH):
            ancestor = lookup(parent_row, ancestor)
            holders.append(lookup(owner_row, ancestor))
        block_ids = jnp.stack(holders).astype(jnp.int32)
        chosen = jnp.stack([lax.dynamic_index_in_dim(blocks3, holder, 0, keepdims=False) for holder in holders])
        start = (position * SEG_LEN).astype(jnp.int32)
        query_rows = lax.dynamic_slice_in_dim(query_all, start, SEG_LEN, 0)
        grad_rows = lax.dynamic_slice_in_dim(grad_all, start, SEG_LEN, 0)
        output, query_grad, slot_grads = attend(query_rows, chosen, level_ok, grad_rows)
        return output, query_grad, slot_grads, block_ids, level_ok

    outputs, query_grads, slot_grads, block_ids, level_ok = lax.map(one_block, seg_ids)
    onehot = ((block_ids[:, :, None] == seg_ids[None, None, :]) & level_ok[:, :, None]).astype(jnp.float32)
    flat = slot_grads.reshape(SEGS, DEPTH, SEG_LEN * 2 * HEAD)
    kv_diff = jnp.einsum('jks,jkr->sr', onehot, flat, precision=lax.Precision.HIGHEST)
    diff_rounded = kv_diff.reshape(SEGS * SEG_LEN, 2 * HEAD).astype(jnp.bfloat16)
    grad = jnp.dot(tokens.T, diff_rounded, preferred_element_type=jnp.float32)
    return outputs.reshape(SEGS * SEG_LEN, HEADS * HEAD), query_grads.reshape(SEGS * SEG_LEN, HEADS * HEAD), grad


def reference(hidden_states, queries, key_value_weight, attention_grad, parents, owners, depths):
    total = jnp.zeros((D, 2 * HEAD), jnp.float32)
    outputs = []
    query_grads = []
    for tree in range(TREES):
        output, query_grad, grad = tree_pass(hidden_states[tree], queries[tree], attention_grad[tree], parents[tree], owners[tree], depths[tree], key_value_weight)
        outputs.append(output)
        query_grads.append(query_grad)
        total = total + grad
    factor = (TREES * SEGS * SEG_LEN) ** -0.5
    return (jnp.stack(outputs), jnp.stack(query_grads), total * factor)
```

```python
import functools

import jax
import jax.numpy as jnp
from jax import lax
from jax.experimental import pallas as pl
from jax.experimental.pallas import tpu as pltpu
from jax.sharding import PartitionSpec as P

HEAD = 128
HEADS = 8
DEPTH = 4
SEGS = 32
SEG_LEN = 256
LEAVES = 8
D = 8192
XS = 4
CHUNK = 2 * SEG_LEN // SEGS
PART = D // LEAVES
F32 = jnp.float32
BF16 = jnp.bfloat16
VMEM_LIMIT = 48 * 1024 * 1024


def smem():
    return pl.BlockSpec(memory_space=pltpu.SMEM)


def vmem():
    return pl.BlockSpec(memory_space=pltpu.VMEM)


def params():
    return pltpu.CompilerParams(vmem_limit_bytes=VMEM_LIMIT)


def shuffle_kernel(where_ref, h_ref, own_ref, other_ref, perm_ref):
    x = where_ref[0]
    core = where_ref[1]

    @pl.when(pl.program_id(0) == 0)
    def _():
        rows = lax.broadcasted_iota(jnp.int32, (512, 512), 0)
        cols = lax.broadcasted_iota(jnp.int32, (512, 512), 1)
        k = cols // 128
        s4 = (cols % 128) // 32
        r = cols % 32
        source = s4 * 128 + ((x + k) % 4) * 32 + r
        perm_ref[...] = jnp.where(rows == source, 1.0, 0.0).astype(BF16)

    for out_ref, half in ((own_ref, core), (other_ref, 1 - core)):
        tiles = [
            h_ref[:, pl.ds(pl.multiple_of(s4 * 256 + half * 128, 128), 128)] for s4 in range(4)
        ]
        picked = jnp.concatenate(tiles, axis=1)
        moved = jnp.dot(picked, perm_ref[...], preferred_element_type=F32).astype(BF16)
        for k in range(XS):
            out_ref[k] = moved[:, k * 128 : (k + 1) * 128]


def shuffle(tokens, where):
    shape = jax.ShapeDtypeStruct((XS, SEG_LEN, PART), BF16)
    spec = pl.BlockSpec((XS, SEG_LEN, 128), lambda g: (0, 0, g))
    return pl.pallas_call(
        shuffle_kernel,
        grid=(D // 1024,),
        in_specs=[smem(), pl.BlockSpec((SEG_LEN, 1024), lambda g: (0, g))],
        out_specs=[spec, spec],
        out_shape=[shape, shape],
        scratch_shapes=[pltpu.VMEM((512, 512), BF16)],
        compiler_params=params(),
        cost_estimate=pl.CostEstimate(
            flops=2 * 2 * SEG_LEN * 512 * 512 * 8, bytes_accessed=8 << 20, transcendentals=0
        ),
    )(where, tokens)


def ancestors_of(parents_ref, seg):
    first = parents_ref[0, seg]
    second = parents_ref[0, first]
    third = parents_ref[0, second]
    return first, second, third


def select_kernel(parents_ref, owners_ref, in_ref, out_ref):
    def step(seg, carry):
        holder = owners_ref[0, seg]
        for k, ancestor in enumerate(ancestors_of(parents_ref, seg)):
            out_ref[holder, k] = in_ref[owners_ref[0, ancestor]]
        return carry

    lax.fori_loop(0, SEGS, step, 0)


def select_chunks(parents, owners, chunks):
    return pl.pallas_call(
        select_kernel,
        in_specs=[smem(), smem(), vmem()],
        out_specs=vmem(),
        out_shape=jax.ShapeDtypeStruct((SEGS, DEPTH - 1, CHUNK, HEAD), BF16),
        compiler_params=params(),
    )(parents, owners, chunks)


def collect_kernel(parents_ref, owners_ref, in_ref, out_ref):
    out_ref[...] = jnp.zeros_like(out_ref)

    def step(seg, carry):
        holder = owners_ref[0, seg]
        for k, ancestor in enumerate(ancestors_of(parents_ref, seg)):
            target = owners_ref[0, ancestor]
            out_ref[target] += in_ref[holder, k]
        return carry

    lax.fori_loop(0, SEGS, step, 0)


def collect_chunks(parents, owners, grads):
    return pl.pallas_call(
        collect_kernel,
        in_specs=[smem(), smem(), vmem()],
        out_specs=vmem(),
        out_shape=jax.ShapeDtypeStruct((SEGS, CHUNK, HEAD), F32),
        compiler_params=params(),
    )(parents, owners, grads)


def dot_nt(a, b):
    return lax.dot_general(a, b, (((1,), (1,)), ((), ())), preferred_element_type=F32)


def dot_nn(a, b):
    return jnp.dot(a, b, preferred_element_type=F32)


def attend_kernel(
    depth_ref, own_ref, anc_ref, q_ref, g_ref,
    out_ref, qgrad_ref, own_grad_ref, anc_grad_ref,
    keys_ref, values_ref, keys_t_ref, values_t_ref, dk_ref, dv_ref,
):
    step = pl.program_id(0)
    factor = HEAD ** (-0.5)
    half = SEGS // 2

    @pl.when(step == 0)
    def _():
        keys_ref[0:SEG_LEN] = own_ref[0:SEG_LEN]
        values_ref[0:SEG_LEN] = own_ref[SEG_LEN : 2 * SEG_LEN]
        for k in range(1, DEPTH):
            rows = slice(k * SEG_LEN, (k + 1) * SEG_LEN)
            keys_ref[rows] = anc_ref[0:half, k - 1].reshape(SEG_LEN, HEAD)
            values_ref[rows] = anc_ref[half:SEGS, k - 1].reshape(SEG_LEN, HEAD)
        keys_t_ref[...] = keys_ref[...].astype(F32).T.astype(BF16)
        values_t_ref[...] = values_ref[...].astype(F32).T.astype(BF16)
        dk_ref[...] = jnp.zeros_like(dk_ref)
        dv_ref[...] = jnp.zeros_like(dv_ref)

    q = q_ref[...]
    g = g_ref[...]
    depth = depth_ref[0]
    key_ids = lax.broadcasted_iota(jnp.int32, (DEPTH * SEG_LEN, SEG_LEN), 0)
    query_ids = lax.broadcasted_iota(jnp.int32, (DEPTH * SEG_LEN, SEG_LEN), 1)
    allowed = (key_ids <= query_ids) | (
        (key_ids >= SEG_LEN) & (key_ids < (depth + 1) * SEG_LEN)
    )
    scores = jnp.where(allowed, dot_nt(keys_ref[...], q) * factor, -jnp.inf)
    peak = jnp.max(scores, axis=0, keepdims=True)
    expd = jnp.exp(scores - peak)
    probs = (expd * (1.0 / jnp.sum(expd, axis=0, keepdims=True))).astype(BF16)
    out_ref[...] = dot_nn(values_t_ref[...], probs).T.astype(BF16)
    dprobs = dot_nt(values_ref[...], g)
    probs_f = probs.astype(F32)
    centre = jnp.sum(probs_f * dprobs, axis=0, keepdims=True)
    dscores = (probs_f * (dprobs - centre)).astype(BF16)
    qgrad_ref[...] = (dot_nn(keys_t_ref[...], dscores).T * factor).astype(BF16)
    dk_ref[...] += dot_nn(dscores, q)
    dv_ref[...] += dot_nn(probs, g)

    @pl.when(step == HEADS - 1)
    def _():
        own_grad_ref[0:SEG_LEN] = dk_ref[0:SEG_LEN] * factor
        own_grad_ref[SEG_LEN : 2 * SEG_LEN] = dv_ref[0:SEG_LEN]
        for k in range(1, DEPTH):
            rows = slice(k * SEG_LEN, (k + 1) * SEG_LEN)
            anc_grad_ref[0:half, k - 1] = (dk_ref[rows] * factor).reshape(half, CHUNK, HEAD)
            anc_grad_ref[half:SEGS, k - 1] = dv_ref[rows].reshape(half, CHUNK, HEAD)


def attend(depth, own, anc, queries, grads):
    head = pl.BlockSpec((SEG_LEN, HEAD), lambda h: (0, h))
    keys = DEPTH * SEG_LEN
    return pl.pallas_call(
        attend_kernel,
        grid=(HEADS,),
        in_specs=[
            smem(),
            pl.BlockSpec((2 * SEG_LEN, HEAD), lambda h: (0, 0)),
            pl.BlockSpec((SEGS, DEPTH - 1, CHUNK, HEAD), lambda h: (0, 0, 0, 0)),
            head,
            head,
        ],
        out_specs=[
            head,
            head,
            pl.BlockSpec((2 * SEG_LEN, HEAD), lambda h: (0, 0)),
            pl.BlockSpec((SEGS, DEPTH - 1, CHUNK, HEAD), lambda h: (0, 0, 0, 0)),
        ],
        out_shape=[
            jax.ShapeDtypeStruct((SEG_LEN, HEADS * HEAD), BF16),
            jax.ShapeDtypeStruct((SEG_LEN, HEADS * HEAD), BF16),
            jax.ShapeDtypeStruct((2 * SEG_LEN, HEAD), F32),
            jax.ShapeDtypeStruct((SEGS, DEPTH - 1, CHUNK, HEAD), F32),
        ],
        scratch_shapes=[
            pltpu.VMEM((keys, HEAD), BF16),
            pltpu.VMEM((keys, HEAD), BF16),
            pltpu.VMEM((HEAD, keys), BF16),
            pltpu.VMEM((HEAD, keys), BF16),
            pltpu.VMEM((keys, HEAD), F32),
            pltpu.VMEM((keys, HEAD), F32),
        ],
        compiler_params=params(),
        cost_estimate=pl.CostEstimate(
            flops=6 * 2 * HEADS * SEG_LEN * keys * HEAD,
            bytes_accessed=6 << 20,
            transcendentals=HEADS * SEG_LEN * keys,
        ),
    )(depth, own, anc, queries, grads)


def x_shift(value, steps):
    pairs = [(i, (i + 2 * steps) % LEAVES) for i in range(LEAVES)]
    return lax.ppermute(value, "leaf", pairs)


def core_swap(value):
    return lax.ppermute(value, "leaf", [(i, i ^ 1) for i in range(LEAVES)])


def over_seg(value):
    return lax.all_to_all(value, "seg", 0, 0, tiled=True)


def per_device(hidden_states, queries, key_value_weight, attention_grad, parents, owners, depths):
    leaf = lax.axis_index("leaf")
    position = lax.axis_index("seg")
    x, core = leaf // 2, leaf % 2
    where = jnp.stack([x, core]).astype(jnp.int32)
    depth = jnp.sum(jnp.where(owners[0] == position, depths[0], 0)).reshape(1)

    piece = lax.dynamic_slice_in_dim(key_value_weight, core * 128 + x * 32, 32, 0)
    weight0 = over_seg(jnp.broadcast_to(piece[None], (SEGS, 32, 2 * HEAD))).reshape(PART, 2 * HEAD)
    weight1 = x_shift(weight0, -1)
    weight3 = x_shift(weight0, 1)
    weight2 = jnp.concatenate(
        [x_shift(weight3[: PART // 2], 1), x_shift(weight1[PART // 2 :], -1)], axis=0
    )
    weights = (weight0, weight1, weight2, weight3)

    mine, other = shuffle(hidden_states[0], where)
    theirs = core_swap(other)

    def project(rows):
        total = 0.0
        for k in (0, 1, 3, 2):
            total = total + dot_nn(rows[k], weights[k])
        return total

    key_values = (project(mine) + core_swap(project(theirs))).astype(BF16)
    stacked = jnp.concatenate([key_values[:, :HEAD], key_values[:, HEAD:]], axis=0)

    mine_later, theirs_later, stacked = lax.optimization_barrier((mine, theirs, stacked))
    columns = [mine_later[0], theirs_later[0]]
    for k in range(1, XS):
        columns.append(x_shift(mine_later[k], k))
        columns.append(x_shift(theirs_later[k], k))

    chunks = over_seg(stacked.reshape(SEGS, CHUNK, HEAD))
    ancestors = over_seg(select_chunks(parents, owners, chunks))
    output, query_grad, own_grad, anc_grad = attend(
        depth, stacked, ancestors, queries[0], attention_grad[0]
    )
    returned = over_seg(collect_chunks(parents, owners, over_seg(anc_grad)))
    diff = (own_grad + returned.reshape(2 * SEG_LEN, HEAD)).astype(BF16)

    diffs = [diff] + [x_shift(diff, k) for k in range(1, XS)]
    swapped = core_swap(jnp.stack(diffs))
    pairs = []
    for k in range(XS):
        pairs.extend([diffs[k], swapped[k]])
    grads = jnp.concatenate(
        [jnp.concatenate([d[:SEG_LEN], d[SEG_LEN:]], axis=1) for d in pairs], axis=0
    )
    total = lax.dot_general(
        jnp.concatenate(columns, axis=0), grads, (((0,), (0,)), ((), ())), preferred_element_type=F32
    )
    summed = jnp.sum(over_seg(total.reshape(SEGS, 32, 2 * HEAD)), axis=0)
    factor = float(LEAVES * SEGS * SEG_LEN) ** (-0.5)
    gathered = lax.all_gather(summed * factor, "leaf", axis=0, tiled=False)
    grad_block = gathered.reshape(XS, 2, 32, 2 * HEAD).transpose(1, 0, 2, 3)
    return (output[None], query_grad[None], grad_block.reshape(SEG_LEN, 2 * HEAD))


def solution(mesh):
    placed = (
        P("leaf", "seg", None),
        P("leaf", "seg", None),
        P("seg", None),
        P("leaf", "seg", None),
        P("leaf", None),
        P("leaf", None),
        P("leaf", None),
    )
    return jax.shard_map(
        per_device,
        mesh=mesh,
        in_specs=placed,
        out_specs=(P("leaf", "seg", None), P("leaf", "seg", None), P("seg", None)),
        check_vma=False,
    )
```

```python
import functools
import math

import jax
import jax.numpy as jnp
from jax import lax
from jax.experimental import pallas as pl
from jax.experimental.pallas import tpu as pltpu
from jax.sharding import PartitionSpec as P

HEAD = 128
HEADS = 8
DEPTH = 4
SEGS = 32
SEG_LEN = 256
LEAVES = 8
D = 8192
XS = 4
ZS = 8
STEP_HEADS = 2
CHUNK = 2 * SEG_LEN // SEGS
PART = D // LEAVES
F32 = jnp.float32
BF16 = jnp.bfloat16
VMEM_LIMIT = 48 * 1024 * 1024


def smem():
    return pl.BlockSpec(memory_space=pltpu.SMEM)


def vmem():
    return pl.BlockSpec(memory_space=pltpu.VMEM)


def params():
    return pltpu.CompilerParams(vmem_limit_bytes=VMEM_LIMIT)


def shuffle_kernel(where_ref, h_ref, *refs):
    own_refs, other_refs, perm_ref = refs[:XS], refs[XS : 2 * XS], refs[2 * XS]
    x, core = where_ref[0], where_ref[1]

    @pl.when(pl.program_id(0) == 0)
    def _():
        rows = lax.broadcasted_iota(jnp.int32, (512, 512), 0)
        cols = lax.broadcasted_iota(jnp.int32, (512, 512), 1)
        k, s4, r = cols >> 7, (cols >> 5) & 3, cols & 31
        source = (s4 << 7) + (((x + k) & 3) << 5) + r
        perm_ref[...] = jnp.where(rows == source, 1.0, 0.0).astype(BF16)

    for out_refs, half in ((own_refs, core), (other_refs, 1 - core)):
        tiles = [
            h_ref[:, pl.ds(pl.multiple_of(s4 * 256 + half * 128, 128), 128)] for s4 in range(4)
        ]
        picked = jnp.concatenate(tiles, axis=1)
        moved = jnp.dot(picked, perm_ref[...], preferred_element_type=F32).astype(BF16)
        for k in range(XS):
            out_refs[k][...] = moved[:, k * 128 : (k + 1) * 128]


def shuffle(tokens, where):
    shape = jax.ShapeDtypeStruct((SEG_LEN, PART), BF16)
    spec = pl.BlockSpec(
        (SEG_LEN, 128), lambda g, where_ref: (0, ((g // 2 - where_ref[2]) & 3) * 2 + g % 2)
    )
    out = pl.pallas_call(
        shuffle_kernel,
        grid_spec=pltpu.PrefetchScalarGridSpec(
            num_scalar_prefetch=1,
            grid=(D // 1024,),
            in_specs=[pl.BlockSpec((SEG_LEN, 1024), lambda g, where_ref: (0, g))],
            out_specs=[spec] * (2 * XS),
            scratch_shapes=[pltpu.VMEM((512, 512), BF16)],
        ),
        out_shape=[shape] * (2 * XS),
        compiler_params=params(),
        cost_estimate=pl.CostEstimate(
            flops=2 * 2 * SEG_LEN * 512 * 512 * 8, bytes_accessed=8 << 20, transcendentals=0
        ),
    )(where, tokens)
    return out[:XS], out[XS:]


def project_kernel(*refs):
    own_refs, their_refs = refs[:XS], refs[XS : 2 * XS]
    by_y, by_x = refs[2 * XS : 2 * XS + 5], refs[2 * XS + 5 : 2 * XS + 10]
    outs = refs[2 * XS + 10 :]
    for rows, out_ref in ((own_refs, outs[0]), (their_refs, outs[1])):

        def tiles(pairs, half):
            return jnp.concatenate(
                [rows[d][:, (2 * e + half) * 128 : (2 * e + half + 1) * 128] for d, e in pairs],
                axis=1,
            )

        total = 0.0
        for n, e in ((0, 0), (1, 1), (2, 3)):
            total = total + dot_nn(tiles([(d, e) for d in range(4)], 0), by_y[n][...])
        for n, d in ((0, 0), (1, 1), (2, 3)):
            total = total + dot_nn(tiles([(d, e) for e in range(4)], 1), by_x[n][...])
        total = total + dot_nn(tiles([(0, 2), (1, 2)], 0), by_y[3][...])
        total = total + dot_nn(tiles([(2, 2), (3, 2)], 0), by_y[4][...])
        total = total + dot_nn(tiles([(2, 0), (2, 1)], 1), by_x[3][...])
        total = total + dot_nn(tiles([(2, 2), (2, 3)], 1), by_x[4][...])
        out_ref[...] = total


def project(mine, theirs, by_y, by_x):
    shape = jax.ShapeDtypeStruct((SEG_LEN, 2 * HEAD), F32)
    return pl.pallas_call(
        project_kernel,
        in_specs=[vmem()] * 18,
        out_specs=[vmem()] * 2,
        out_shape=[shape] * 2,
        compiler_params=params(),
        cost_estimate=pl.CostEstimate(
            flops=2 * 2 * SEG_LEN * D // 2 * 2 * HEAD, bytes_accessed=7 << 20, transcendentals=0
        ),
    )(*mine, *theirs, *by_y, *by_x)


def gradient_kernel(*refs):
    total = 0.0
    for t_ref, d_ref in zip(refs[:LEAVES], refs[LEAVES : 2 * LEAVES]):
        both = jnp.concatenate([d_ref[0:SEG_LEN], d_ref[SEG_LEN : 2 * SEG_LEN]], axis=1)
        total = total + dot_nn(both.T, t_ref[...])
    refs[2 * LEAVES][...] = total.T


def gradient(columns, diffs, block):
    return pl.pallas_call(
        gradient_kernel,
        grid=(1,),
        in_specs=[pl.BlockSpec((SEG_LEN, SEG_LEN), lambda i: (0, block))] * LEAVES
        + [pl.BlockSpec((2 * SEG_LEN, HEAD), lambda i: (0, 0))] * LEAVES,
        out_specs=pl.BlockSpec((SEG_LEN, 2 * HEAD), lambda i: (0, 0)),
        out_shape=jax.ShapeDtypeStruct((SEG_LEN, 2 * HEAD), F32),
        compiler_params=params(),
        cost_estimate=pl.CostEstimate(
            flops=2 * LEAVES * SEG_LEN * SEG_LEN * 2 * HEAD, bytes_accessed=3 << 20, transcendentals=0
        ),
    )(*columns, *diffs)


def place_kernel(where_ref, *refs):
    x, core = where_ref[0], where_ref[1]
    for k in range(XS):
        plane = (x - k) & 3
        for n, half in ((k, core), (XS + k, 1 - core)):
            refs[2 * XS][pl.ds(pl.multiple_of((half * 4 + plane) * 32, 32), 32), :] = refs[n][...]


def place(where, same, swapped):
    return pl.pallas_call(
        place_kernel,
        in_specs=[smem()] + [vmem()] * (2 * XS),
        out_specs=vmem(),
        out_shape=jax.ShapeDtypeStruct((SEG_LEN, 2 * HEAD), F32),
        compiler_params=params(),
    )(where, *same, *swapped)


def ancestors_of(parents_ref, seg):
    first = parents_ref[0, seg]
    second = parents_ref[0, first]
    third = parents_ref[0, second]
    return first, second, third


def select_kernel(parents_ref, owners_ref, in_ref, out_ref):
    def step(seg, carry):
        holder = owners_ref[0, seg]
        for k, ancestor in enumerate(ancestors_of(parents_ref, seg)):
            out_ref[holder, k] = in_ref[owners_ref[0, ancestor]]
        return carry

    lax.fori_loop(0, SEGS, step, 0)


def select_chunks(parents, owners, chunks):
    return pl.pallas_call(
        select_kernel,
        in_specs=[smem(), smem(), vmem()],
        out_specs=vmem(),
        out_shape=jax.ShapeDtypeStruct((SEGS, DEPTH - 1, CHUNK, HEAD), BF16),
        compiler_params=params(),
    )(parents, owners, chunks)


def collect_kernel(parents_ref, owners_ref, in_ref, out_ref):
    out_ref[...] = jnp.zeros_like(out_ref)

    def step(seg, carry):
        holder = owners_ref[0, seg]
        for k, ancestor in enumerate(ancestors_of(parents_ref, seg)):
            target = owners_ref[0, ancestor]
            out_ref[target] += in_ref[holder, k].astype(F32)
        return carry

    lax.fori_loop(0, SEGS, step, 0)


def collect_chunks(parents, owners, grads):
    return pl.pallas_call(
        collect_kernel,
        in_specs=[smem(), smem(), vmem()],
        out_specs=vmem(),
        out_shape=jax.ShapeDtypeStruct((SEGS, CHUNK, HEAD), F32),
        compiler_params=params(),
    )(parents, owners, grads)


def dot_nt(a, b):
    return lax.dot_general(a, b, (((1,), (1,)), ((), ())), preferred_element_type=F32)


def dot_nn(a, b):
    return jnp.dot(a, b, preferred_element_type=F32)


def attend_kernel(
    depth_ref, own_ref, anc_ref, q_ref, g_ref,
    out_ref, qgrad_ref, own_grad_ref, anc_grad_ref,
    keys_ref, values_ref, keys_t_ref, values_t_ref, dk_ref, dv_ref,
):
    step = pl.program_id(0)
    factor = HEAD ** (-0.5)
    log2_factor = factor * math.log2(math.e)
    half = SEGS // 2
    blocks = [slice(b * SEG_LEN, (b + 1) * SEG_LEN) for b in range(DEPTH)]

    @pl.when(step == 0)
    def _():
        keys_ref[blocks[0]] = own_ref[0:SEG_LEN]
        values_ref[blocks[0]] = own_ref[SEG_LEN : 2 * SEG_LEN]
        for b in range(1, DEPTH):
            keys_ref[blocks[b]] = anc_ref[0:half, b - 1].reshape(SEG_LEN, HEAD)
            values_ref[blocks[b]] = anc_ref[half:SEGS, b - 1].reshape(SEG_LEN, HEAD)
        keys_t_ref[...] = keys_ref[...].T
        values_t_ref[...] = values_ref[...].T
        dk_ref[...] = jnp.zeros_like(dk_ref)
        dv_ref[...] = jnp.zeros_like(dv_ref)

    depth = depth_ref[0]
    causal = lax.broadcasted_iota(jnp.int32, (SEG_LEN, SEG_LEN), 0) <= lax.broadcasted_iota(
        jnp.int32, (SEG_LEN, SEG_LEN), 1
    )
    for h in range(STEP_HEADS):
        cols = slice(h * HEAD, (h + 1) * HEAD)
        q = q_ref[:, cols]
        g = g_ref[:, cols]
        scores = []
        for b in range(DEPTH):
            block = dot_nt(keys_ref[blocks[b]], q)
            if b == 0:
                block = jnp.where(causal, block, -jnp.inf)
            else:
                block = block + jnp.where(depth >= b, 0.0, -jnp.inf)
            scores.append(block)
        peak = jnp.max(functools.reduce(jnp.maximum, scores), axis=0, keepdims=True) * log2_factor
        expd = [jnp.exp2(block * log2_factor - peak) for block in scores]
        scale = 1.0 / sum(jnp.sum(block, axis=0, keepdims=True) for block in expd)
        probs = [(block * scale).astype(BF16) for block in expd]
        dprobs = [dot_nt(values_ref[blocks[b]], g) for b in range(DEPTH)]
        centre = sum(
            jnp.sum(p.astype(F32) * dp, axis=0, keepdims=True) for p, dp in zip(probs, dprobs)
        )
        dscores = [(p.astype(F32) * (dp - centre)).astype(BF16) for p, dp in zip(probs, dprobs)]
        probs = jnp.concatenate(probs, axis=0)
        dscores = jnp.concatenate(dscores, axis=0)
        out_ref[:, cols] = dot_nn(values_t_ref[...], probs).T.astype(BF16)
        qgrad_ref[:, cols] = (dot_nn(keys_t_ref[...], dscores).T * factor).astype(BF16)
        dk_ref[...] += dot_nn(dscores, q)
        dv_ref[...] += dot_nn(probs, g)

    @pl.when(step == HEADS // STEP_HEADS - 1)
    def _():
        own_grad_ref[0:SEG_LEN] = dk_ref[blocks[0]] * factor
        own_grad_ref[SEG_LEN : 2 * SEG_LEN] = dv_ref[blocks[0]]
        for b in range(1, DEPTH):
            anc_grad_ref[0:half, b - 1] = (
                (dk_ref[blocks[b]] * factor).astype(BF16).reshape(half, CHUNK, HEAD)
            )
            anc_grad_ref[half:SEGS, b - 1] = (
                dv_ref[blocks[b]].astype(BF16).reshape(half, CHUNK, HEAD)
            )


def attend(depth, own, anc, queries, grads):
    head = pl.BlockSpec((SEG_LEN, STEP_HEADS * HEAD), lambda h: (0, h))
    keys = DEPTH * SEG_LEN
    return pl.pallas_call(
        attend_kernel,
        grid=(HEADS // STEP_HEADS,),
        in_specs=[
            smem(),
            pl.BlockSpec((2 * SEG_LEN, HEAD), lambda h: (0, 0)),
            pl.BlockSpec((SEGS, DEPTH - 1, CHUNK, HEAD), lambda h: (0, 0, 0, 0)),
            head,
            head,
        ],
        out_specs=[
            head,
            head,
            pl.BlockSpec((2 * SEG_LEN, HEAD), lambda h: (0, 0)),
            pl.BlockSpec((SEGS, DEPTH - 1, CHUNK, HEAD), lambda h: (0, 0, 0, 0)),
        ],
        out_shape=[
            jax.ShapeDtypeStruct((SEG_LEN, HEADS * HEAD), BF16),
            jax.ShapeDtypeStruct((SEG_LEN, HEADS * HEAD), BF16),
            jax.ShapeDtypeStruct((2 * SEG_LEN, HEAD), F32),
            jax.ShapeDtypeStruct((SEGS, DEPTH - 1, CHUNK, HEAD), BF16),
        ],
        scratch_shapes=[
            pltpu.VMEM((keys, HEAD), BF16),
            pltpu.VMEM((keys, HEAD), BF16),
            pltpu.VMEM((HEAD, keys), BF16),
            pltpu.VMEM((HEAD, keys), BF16),
            pltpu.VMEM((keys, HEAD), F32),
            pltpu.VMEM((keys, HEAD), F32),
        ],
        compiler_params=params(),
        cost_estimate=pl.CostEstimate(
            flops=6 * 2 * HEADS * SEG_LEN * keys * HEAD,
            bytes_accessed=6 << 20,
            transcendentals=HEADS * SEG_LEN * keys,
        ),
    )(depth, own, anc, queries, grads)


def x_shift(value, steps, flip=0):
    pairs = [(i, ((i + 2 * steps) % LEAVES) ^ flip) for i in range(LEAVES)]
    return lax.ppermute(value, "leaf", pairs)


def core_swap(value):
    return x_shift(value, 0, 1)


def y_shift(value, steps):
    return lax.ppermute(value, "seg", [(i, (i + ZS * steps) % SEGS) for i in range(SEGS)])


def over_z(value):
    groups = [list(range(i, i + ZS)) for i in range(0, SEGS, ZS)]
    return lax.all_to_all(value, "seg", 0, 0, axis_index_groups=groups, tiled=True)


def over_seg(value):
    return lax.all_to_all(value, "seg", 0, 0, tiled=True)


def ring(shift, value):
    return jnp.concatenate([value] + [shift(value, -d) for d in range(1, 4)], axis=0)


def ring_halves(shift, value):
    half = value.shape[0] // 2
    ahead, behind = shift(value, -1), shift(value, 1)
    return value, ahead, behind, shift(behind[:half], 1), shift(ahead[half:], -1)


def per_device(hidden_states, queries, key_value_weight, attention_grad, parents, owners, depths):
    leaf = lax.axis_index("leaf")
    position = lax.axis_index("seg")
    x, core, y = leaf // 2, leaf % 2, position // ZS
    where = jnp.stack([x, core, y]).astype(jnp.int32)
    depth = jnp.sum(jnp.where(owners[0] == position, depths[0], 0)).reshape(1)

    piece = lax.dynamic_slice_in_dim(key_value_weight, core * 128 + x * 32, 32, 0)
    column = over_z(jnp.broadcast_to(piece[None], (ZS, 32, 2 * HEAD))).reshape(ZS * 32, 2 * HEAD)
    by_y = ring_halves(y_shift, ring(x_shift, column[: ZS * 16]))
    by_x = ring_halves(x_shift, ring(y_shift, column[ZS * 16 :]))

    mine, other = shuffle(hidden_states[0], where)
    theirs = [core_swap(block) for block in other]
    own_part, their_part = project(mine, theirs, by_y, by_x)
    key_values = (own_part + core_swap(their_part)).astype(BF16)
    stacked = jnp.concatenate([key_values[:, :HEAD], key_values[:, HEAD:]], axis=0)

    mine, other, _ = lax.optimization_barrier((mine, other, own_part))
    columns = {0: (mine[0], theirs[0])}
    for k in (1, 3, 2):
        columns[k] = (x_shift(mine[k], k), x_shift(other[k], k, 1))

    chunks = over_seg(stacked.reshape(SEGS, CHUNK, HEAD))
    ancestors = over_seg(select_chunks(parents, owners, chunks))
    ancestors, columns[1], columns[3] = lax.optimization_barrier(
        (ancestors, columns[1], columns[3])
    )
    output, query_grad, own_grad, anc_grad = attend(
        depth, stacked, ancestors, queries[0], attention_grad[0]
    )
    arrived, columns[2] = lax.optimization_barrier((over_seg(anc_grad), columns[2]))
    returned = over_seg(collect_chunks(parents, owners, arrived))
    diff = (own_grad + returned.reshape(2 * SEG_LEN, HEAD)).astype(BF16)

    diffs = [diff] + [x_shift(diff, k) for k in range(1, XS)]
    swapped = [core_swap(d) for d in diffs]
    ordered = [columns[k][n] for k in range(XS) for n in range(2)]
    pairs = [d for k in range(XS) for d in (diffs[k], swapped[k])]
    blocks = {e: gradient(ordered, pairs, e) for e in (2, 1, 3, 0)}
    summed = blocks[0]
    for e in (1, 3, 2):
        summed = summed + y_shift(blocks[e], e)
    factor = float(LEAVES * SEGS * SEG_LEN) ** (-0.5)
    share = jnp.sum(over_z(summed.reshape(ZS, 32, 2 * HEAD)), axis=0) * factor
    shares = [share] + [x_shift(share, k) for k in range(1, XS)]
    grad_block = place(where, shares, [core_swap(s) for s in shares])
    return (output[None], query_grad[None], grad_block)


def solution(mesh):
    placed = (
        P("leaf", "seg", None),
        P("leaf", "seg", None),
        P("seg", None),
        P("leaf", "seg", None),
        P("leaf", None),
        P("leaf", None),
        P("leaf", None),
    )
    return jax.shard_map(
        per_device,
        mesh=mesh,
        in_specs=placed,
        out_specs=(P("leaf", "seg", None), P("leaf", "seg", None), P("seg", None)),
        check_vma=False,
    )
```

```python
import functools
import math

import jax
import jax.numpy as jnp
from jax import lax
from jax.experimental import pallas as pl
from jax.experimental.pallas import tpu as pltpu
from jax.sharding import PartitionSpec as P

HEAD = 128
HEADS = 8
DEPTH = 4
SEGS = 32
SEG_LEN = 256
LEAVES = 8
D = 8192
XS = 4
ZS = 8
STEP_HEADS = 2
CHUNK = 2 * SEG_LEN // SEGS
PART = D // LEAVES
F32 = jnp.float32
BF16 = jnp.bfloat16
VMEM_LIMIT = 40 * 1024 * 1024
VMEM_MOST = 60 * 1024 * 1024


def smem():
    return pl.BlockSpec(memory_space=pltpu.SMEM)


def vmem():
    return pl.BlockSpec(memory_space=pltpu.VMEM)


def params(limit=VMEM_LIMIT):
    return pltpu.CompilerParams(vmem_limit_bytes=limit)


def shuffle_kernel(where_ref, h_ref, theirs_ref, both0, own1, theirs1, both2, own3, theirs3, perm_ref):
    x, core = where_ref[0], where_ref[1]

    @pl.when(pl.program_id(0) == 0)
    def _():
        rows = lax.broadcasted_iota(jnp.int32, (512, 512), 0)
        cols = lax.broadcasted_iota(jnp.int32, (512, 512), 1)
        k, s4, r = cols >> 7, (cols >> 5) & 3, cols & 31
        source = (s4 << 7) + (((x + k) & 3) << 5) + r
        perm_ref[...] = jnp.where(rows == source, 1.0, 0.0).astype(BF16)

    top, bottom = slice(0, SEG_LEN), slice(SEG_LEN, 2 * SEG_LEN)
    for half in range(2):
        lanes = slice(half * 128, (half + 1) * 128)
        for in_ref, rows, one1, one3 in (
            (h_ref, top, own1, own3),
            (theirs_ref, bottom, theirs1, theirs3),
        ):
            tiles = [
                in_ref[:, pl.ds(pl.multiple_of((half * 4 + s4) * 256 + core * 128, 128), 128)]
                for s4 in range(4)
            ]
            moved = jnp.dot(
                jnp.concatenate(tiles, axis=1), perm_ref[...], preferred_element_type=F32
            ).astype(BF16)
            both0[rows, lanes] = moved[:, 0:128]
            one1[:, lanes] = moved[:, 128:256]
            both2[rows, lanes] = moved[:, 256:384]
            one3[:, lanes] = moved[:, 384:512]


def shuffle(tokens, theirs, where):
    both = jax.ShapeDtypeStruct((2 * SEG_LEN, PART), BF16)
    one = jax.ShapeDtypeStruct((SEG_LEN, PART), BF16)
    both_spec = pl.BlockSpec((2 * SEG_LEN, 256), lambda g, where_ref: (0, (g - where_ref[2]) & 3))
    one_spec = pl.BlockSpec((SEG_LEN, 256), lambda g, where_ref: (0, (g - where_ref[2]) & 3))
    raw = pl.BlockSpec((SEG_LEN, 2048), lambda g, where_ref: (0, g))
    return pl.pallas_call(
        shuffle_kernel,
        grid_spec=pltpu.PrefetchScalarGridSpec(
            num_scalar_prefetch=1,
            grid=(D // 2048,),
            in_specs=[raw, raw],
            out_specs=[both_spec, one_spec, one_spec] * 2,
            scratch_shapes=[pltpu.VMEM((512, 512), BF16)],
        ),
        out_shape=[both, one, one] * 2,
        compiler_params=params(VMEM_MOST),
        cost_estimate=pl.CostEstimate(
            flops=2 * 2 * SEG_LEN * 512 * 512 * 8, bytes_accessed=12 << 20, transcendentals=0
        ),
    )(where, tokens, theirs)


def row_blocks(refs):
    both0, own1, theirs1, both2, own3, theirs3 = refs
    top, bottom = slice(0, SEG_LEN), slice(SEG_LEN, 2 * SEG_LEN)
    return (
        (both0[top], both0[bottom]),
        (own1[...], theirs1[...]),
        (both2[top], both2[bottom]),
        (own3[...], theirs3[...]),
    )


def column_specs(block=None):
    def index(step):
        return (0, step if block is None else block)

    both_spec = pl.BlockSpec((2 * SEG_LEN, 256), index)
    one_spec = pl.BlockSpec((SEG_LEN, 256), index)
    return [both_spec, one_spec, one_spec] * 2


def project_kernel(where_ref, *refs):
    columns, (w0, w1, w3, w2a, w2b), (own_ref, their_ref) = refs[:6], refs[6:11], refs[11:]
    x = where_ref[0]
    step = pl.program_id(0)

    def part(k, z_refs):
        start = pl.multiple_of(((x + k) & 3) * 32, 32)
        return jnp.concatenate([ref[z, pl.ds(start, 32), :] for ref, z in z_refs], axis=0)

    for n, ref in enumerate((w0, w1, None, w3)):

        @pl.when(step == n)
        def _():
            if ref is None:
                z_refs = [(w2a, z) for z in range(4)] + [(w2b, z) for z in range(4)]
            else:
                z_refs = [(ref, z) for z in range(ZS)]
            own, theirs = 0.0, 0.0
            for k, (own_rows, their_rows) in enumerate(row_blocks(columns)):
                weight = part(k, z_refs)
                own = own + dot_nn(own_rows, weight)
                theirs = theirs + dot_nn(their_rows, weight)
            if n == 0:
                own_ref[...] = own
                their_ref[...] = theirs
            else:
                own_ref[...] += own
                their_ref[...] += theirs


def project(where, rows, weights):
    shape = jax.ShapeDtypeStruct((SEG_LEN, 2 * HEAD), F32)
    return pl.pallas_call(
        project_kernel,
        grid=(4,),
        in_specs=[smem()] + column_specs() + [vmem()] * 5,
        out_specs=[pl.BlockSpec((SEG_LEN, 2 * HEAD), lambda e: (0, 0))] * 2,
        out_shape=[shape] * 2,
        compiler_params=params(VMEM_MOST),
        cost_estimate=pl.CostEstimate(
            flops=2 * 2 * SEG_LEN * D // 2 * 2 * HEAD, bytes_accessed=7 << 20, transcendentals=0
        ),
    )(where, *rows, *weights)


def stack_kernel(a_ref, b_ref, out_ref):
    total = (a_ref[...] + b_ref[...]).astype(BF16)
    out_ref[0:SEG_LEN] = total[:, :HEAD]
    out_ref[SEG_LEN : 2 * SEG_LEN] = total[:, HEAD:]


def stack(a, b):
    return pl.pallas_call(
        stack_kernel,
        in_specs=[vmem()] * 2,
        out_specs=vmem(),
        out_shape=jax.ShapeDtypeStruct((2 * SEG_LEN, HEAD), BF16),
        compiler_params=params(),
    )(a, b)


def gradient_kernel(*refs):
    columns, diffs, out_ref = refs[:6], refs[6:14], refs[14]
    blocks = [block for pair in row_blocks(columns) for block in pair]
    total = 0.0
    for block, d_ref in zip(blocks, diffs):
        both = jnp.concatenate([d_ref[0:SEG_LEN], d_ref[SEG_LEN : 2 * SEG_LEN]], axis=1)
        total = total + dot_nn(both.T, block)
    out_ref[...] = total.T


def gradient(columns, diffs, block):
    return pl.pallas_call(
        gradient_kernel,
        grid=(1,),
        in_specs=column_specs(block)
        + [pl.BlockSpec((2 * SEG_LEN, HEAD), lambda i: (0, 0))] * LEAVES,
        out_specs=pl.BlockSpec((SEG_LEN, 2 * HEAD), lambda i: (0, 0)),
        out_shape=jax.ShapeDtypeStruct((SEG_LEN, 2 * HEAD), F32),
        compiler_params=params(),
        cost_estimate=pl.CostEstimate(
            flops=2 * LEAVES * SEG_LEN * SEG_LEN * 2 * HEAD, bytes_accessed=3 << 20, transcendentals=0
        ),
    )(*columns, *diffs)


def place_kernel(where_ref, *refs):
    x, core = where_ref[0], where_ref[1]
    for k in range(XS):
        plane = (x - k) & 3
        for n, half in ((k, core), (XS + k, 1 - core)):
            refs[2 * XS][pl.ds(pl.multiple_of((half * 4 + plane) * 32, 32), 32), :] = refs[n][...]


def place(where, same, swapped):
    return pl.pallas_call(
        place_kernel,
        in_specs=[smem()] + [vmem()] * (2 * XS),
        out_specs=vmem(),
        out_shape=jax.ShapeDtypeStruct((SEG_LEN, 2 * HEAD), F32),
        compiler_params=params(),
    )(where, *same, *swapped)


def ancestors_of(parents_ref, seg):
    first = parents_ref[0, seg]
    second = parents_ref[0, first]
    third = parents_ref[0, second]
    return first, second, third


def select_kernel(parents_ref, owners_ref, in_ref, out_ref):
    def step(seg, carry):
        holder = owners_ref[0, seg]
        for k, ancestor in enumerate(ancestors_of(parents_ref, seg)):
            out_ref[holder, k] = in_ref[owners_ref[0, ancestor]]
        return carry

    lax.fori_loop(0, SEGS, step, 0)


def select_chunks(parents, owners, chunks):
    return pl.pallas_call(
        select_kernel,
        in_specs=[smem(), smem(), vmem()],
        out_specs=vmem(),
        out_shape=jax.ShapeDtypeStruct((SEGS, DEPTH - 1, CHUNK, HEAD), BF16),
        compiler_params=params(),
    )(parents, owners, chunks)


def collect_kernel(parents_ref, owners_ref, in_ref, out_ref):
    out_ref[...] = jnp.zeros_like(out_ref)

    def step(seg, carry):
        holder = owners_ref[0, seg]
        for k, ancestor in enumerate(ancestors_of(parents_ref, seg)):
            target = owners_ref[0, ancestor]
            out_ref[target] += in_ref[holder, k].astype(F32)
        return carry

    lax.fori_loop(0, SEGS, step, 0)


def collect_chunks(parents, owners, grads):
    return pl.pallas_call(
        collect_kernel,
        in_specs=[smem(), smem(), vmem()],
        out_specs=vmem(),
        out_shape=jax.ShapeDtypeStruct((SEGS, CHUNK, HEAD), F32),
        compiler_params=params(),
    )(parents, owners, grads)


def dot_nt(a, b):
    return lax.dot_general(a, b, (((1,), (1,)), ((), ())), preferred_element_type=F32)


def dot_nn(a, b):
    return jnp.dot(a, b, preferred_element_type=F32)


def attend_kernel(
    depth_ref, own_ref, anc_ref, q_ref, g_ref,
    out_ref, qgrad_ref, own_grad_ref, anc_grad_ref,
    keys_ref, values_ref, keys_t_ref, values_t_ref, dk_ref, dv_ref,
):
    step = pl.program_id(0)
    factor = HEAD ** (-0.5)
    log2_factor = factor * math.log2(math.e)
    half = SEGS // 2
    blocks = [slice(b * SEG_LEN, (b + 1) * SEG_LEN) for b in range(DEPTH)]

    @pl.when(step == 0)
    def _():
        keys_ref[blocks[0]] = own_ref[0:SEG_LEN]
        values_ref[blocks[0]] = own_ref[SEG_LEN : 2 * SEG_LEN]
        for b in range(1, DEPTH):
            keys_ref[blocks[b]] = anc_ref[0:half, b - 1].reshape(SEG_LEN, HEAD)
            values_ref[blocks[b]] = anc_ref[half:SEGS, b - 1].reshape(SEG_LEN, HEAD)
        keys_t_ref[...] = keys_ref[...].T
        values_t_ref[...] = values_ref[...].T
        dk_ref[...] = jnp.zeros_like(dk_ref)
        dv_ref[...] = jnp.zeros_like(dv_ref)

    depth = depth_ref[0]
    causal = lax.broadcasted_iota(jnp.int32, (SEG_LEN, SEG_LEN), 0) <= lax.broadcasted_iota(
        jnp.int32, (SEG_LEN, SEG_LEN), 1
    )
    for h in range(STEP_HEADS):
        cols = slice(h * HEAD, (h + 1) * HEAD)
        q = q_ref[:, cols]
        g = g_ref[:, cols]
        scores = []
        for b in range(DEPTH):
            block = dot_nt(keys_ref[blocks[b]], q)
            if b == 0:
                block = jnp.where(causal, block, -jnp.inf)
            else:
                block = block + jnp.where(depth >= b, 0.0, -jnp.inf)
            scores.append(block)
        peak = jnp.max(functools.reduce(jnp.maximum, scores), axis=0, keepdims=True) * log2_factor
        expd = [jnp.exp2(block * log2_factor - peak) for block in scores]
        scale = 1.0 / sum(jnp.sum(block, axis=0, keepdims=True) for block in expd)
        probs = [(block * scale).astype(BF16) for block in expd]
        dprobs = [dot_nt(values_ref[blocks[b]], g) for b in range(DEPTH)]
        centre = sum(
            jnp.sum(p.astype(F32) * dp, axis=0, keepdims=True) for p, dp in zip(probs, dprobs)
        )
        dscores = [(p.astype(F32) * (dp - centre)).astype(BF16) for p, dp in zip(probs, dprobs)]
        probs = jnp.concatenate(probs, axis=0)
        dscores = jnp.concatenate(dscores, axis=0)
        out_ref[:, cols] = dot_nn(values_t_ref[...], probs).T.astype(BF16)
        qgrad_ref[:, cols] = (dot_nn(keys_t_ref[...], dscores).T * factor).astype(BF16)
        dk_ref[...] += dot_nn(dscores, q)
        dv_ref[...] += dot_nn(probs, g)

    @pl.when(step == HEADS // STEP_HEADS - 1)
    def _():
        own_grad_ref[0:SEG_LEN] = dk_ref[blocks[0]] * factor
        own_grad_ref[SEG_LEN : 2 * SEG_LEN] = dv_ref[blocks[0]]
        for b in range(1, DEPTH):
            anc_grad_ref[0:half, b - 1] = (
                (dk_ref[blocks[b]] * factor).astype(BF16).reshape(half, CHUNK, HEAD)
            )
            anc_grad_ref[half:SEGS, b - 1] = (
                dv_ref[blocks[b]].astype(BF16).reshape(half, CHUNK, HEAD)
            )


def attend(depth, own, anc, queries, grads):
    head = pl.BlockSpec((SEG_LEN, STEP_HEADS * HEAD), lambda h: (0, h))
    keys = DEPTH * SEG_LEN
    return pl.pallas_call(
        attend_kernel,
        grid=(HEADS // STEP_HEADS,),
        in_specs=[
            smem(),
            pl.BlockSpec((2 * SEG_LEN, HEAD), lambda h: (0, 0)),
            pl.BlockSpec((SEGS, DEPTH - 1, CHUNK, HEAD), lambda h: (0, 0, 0, 0)),
            head,
            head,
        ],
        out_specs=[
            head,
            head,
            pl.BlockSpec((2 * SEG_LEN, HEAD), lambda h: (0, 0)),
            pl.BlockSpec((SEGS, DEPTH - 1, CHUNK, HEAD), lambda h: (0, 0, 0, 0)),
        ],
        out_shape=[
            jax.ShapeDtypeStruct((SEG_LEN, HEADS * HEAD), BF16),
            jax.ShapeDtypeStruct((SEG_LEN, HEADS * HEAD), BF16),
            jax.ShapeDtypeStruct((2 * SEG_LEN, HEAD), F32),
            jax.ShapeDtypeStruct((SEGS, DEPTH - 1, CHUNK, HEAD), BF16),
        ],
        scratch_shapes=[
            pltpu.VMEM((keys, HEAD), BF16),
            pltpu.VMEM((keys, HEAD), BF16),
            pltpu.VMEM((HEAD, keys), BF16),
            pltpu.VMEM((HEAD, keys), BF16),
            pltpu.VMEM((keys, HEAD), F32),
            pltpu.VMEM((keys, HEAD), F32),
        ],
        compiler_params=params(VMEM_MOST),
        cost_estimate=pl.CostEstimate(
            flops=6 * 2 * HEADS * SEG_LEN * keys * HEAD,
            bytes_accessed=6 << 20,
            transcendentals=HEADS * SEG_LEN * keys,
        ),
    )(depth, own, anc, queries, grads)


def x_shift(value, steps, flip=0):
    pairs = [(i, ((i + 2 * steps) % LEAVES) ^ flip) for i in range(LEAVES)]
    return lax.ppermute(value, "leaf", pairs)


def core_swap(value):
    return x_shift(value, 0, 1)


def y_shift(value, steps):
    return lax.ppermute(value, "seg", [(i, (i + ZS * steps) % SEGS) for i in range(SEGS)])


def over_z(value):
    groups = [list(range(i, i + ZS)) for i in range(0, SEGS, ZS)]
    return lax.all_to_all(value, "seg", 0, 0, axis_index_groups=groups, tiled=True)


def over_seg(value):
    return lax.all_to_all(value, "seg", 0, 0, tiled=True)


def per_device(hidden_states, queries, key_value_weight, attention_grad, parents, owners, depths):
    leaf = lax.axis_index("leaf")
    position = lax.axis_index("seg")
    x, core, y = leaf // 2, leaf % 2, position // ZS
    where = jnp.stack([x, core, y]).astype(jnp.int32)
    depth = jnp.sum(jnp.where(owners[0] == position, depths[0], 0)).reshape(1)

    tokens = hidden_states[0]
    half = lax.dynamic_slice_in_dim(key_value_weight, core * 128, 128, 0)
    weight0 = over_z(jnp.broadcast_to(half[None], (ZS, 128, 2 * HEAD)))
    weight0, theirs = lax.optimization_barrier((weight0, core_swap(tokens)))
    weight1, weight3 = y_shift(weight0, -1), y_shift(weight0, 1)
    weight1, weight3, rows = lax.optimization_barrier(
        (weight1, weight3, shuffle(tokens, theirs, where))
    )
    weight2 = y_shift(weight3[:4], 1), y_shift(weight1[4:], -1)

    columns = list(rows)
    columns[1], columns[4] = x_shift(rows[1], 1), x_shift(rows[4], 3)
    weight2, columns = lax.optimization_barrier((weight2, columns))
    own_part, their_part = project(where, rows, (weight0, weight1, weight3, *weight2))
    columns[2], columns[5] = x_shift(rows[2], 1), x_shift(rows[5], 3)
    columns[3] = x_shift(rows[3], 2)
    stacked = stack(own_part, core_swap(their_part))

    def settle(value, *places):
        value, got = lax.optimization_barrier((value, [columns[n] for n in places]))
        for n, block in zip(places, got):
            columns[n] = block
        return value

    chunks = settle(over_seg(stacked.reshape(SEGS, CHUNK, HEAD)), 2, 5)
    ancestors = settle(over_seg(select_chunks(parents, owners, chunks)), 3)
    output, query_grad, own_grad, anc_grad = attend(
        depth, stacked, ancestors, queries[0], attention_grad[0]
    )
    arrived = over_seg(anc_grad)
    returned = over_seg(collect_chunks(parents, owners, arrived))
    diff = (own_grad + returned.reshape(2 * SEG_LEN, HEAD)).astype(BF16)

    diffs = [diff] + [x_shift(diff, k) for k in range(1, XS)]
    swapped = [core_swap(d) for d in diffs]
    pairs = [d for k in range(XS) for d in (diffs[k], swapped[k])]
    blocks = {e: gradient(columns, pairs, e) for e in (2, 1, 3, 0)}
    summed = blocks[0]
    for e in (1, 3, 2):
        summed = summed + y_shift(blocks[e], e)
    factor = float(LEAVES * SEGS * SEG_LEN) ** (-0.5)
    share = jnp.sum(over_z(summed.reshape(ZS, 32, 2 * HEAD)), axis=0) * factor
    shares = [share] + [x_shift(share, k) for k in range(1, XS)]
    grad_block = place(where, shares, [core_swap(s) for s in shares])
    return (output[None], query_grad[None], grad_block)


def solution(mesh):
    placed = (
        P("leaf", "seg", None),
        P("leaf", "seg", None),
        P("seg", None),
        P("leaf", "seg", None),
        P("leaf", None),
        P("leaf", None),
        P("leaf", None),
    )
    return jax.shard_map(
        per_device,
        mesh=mesh,
        in_specs=placed,
        out_specs=(P("leaf", "seg", None), P("leaf", "seg", None), P("seg", None)),
        check_vma=False,
    )
```

```python
import functools
import math

import jax
import jax.numpy as jnp
from jax import lax
from jax.experimental import pallas as pl
from jax.experimental.pallas import tpu as pltpu
from jax.sharding import PartitionSpec as P

HEAD = 128
HEADS = 8
DEPTH = 4
SEGS = 32
SEG_LEN = 256
LEAVES = 8
D = 8192
XS = 4
ZS = 8
STEP_HEADS = 2
CHUNK = 2 * SEG_LEN // SEGS
PART = D // LEAVES
F32 = jnp.float32
BF16 = jnp.bfloat16
VMEM_LIMIT = 40 * 1024 * 1024
VMEM_MOST = 60 * 1024 * 1024
VMEM_LITTLE = 16 * 1024 * 1024


def smem():
    return pl.BlockSpec(memory_space=pltpu.SMEM)


def vmem():
    return pl.BlockSpec(memory_space=pltpu.VMEM)


def params(limit=VMEM_LIMIT):
    return pltpu.CompilerParams(vmem_limit_bytes=limit)


def shuffle_kernel(where_ref, h_ref, theirs_ref, both0, own1, theirs1, both2, own3, theirs3, perm_ref):
    x, core = where_ref[0], where_ref[1]

    @pl.when(pl.program_id(0) == 0)
    def _():
        rows = lax.broadcasted_iota(jnp.int32, (512, 512), 0)
        cols = lax.broadcasted_iota(jnp.int32, (512, 512), 1)
        k, s4, r = cols >> 7, (cols >> 5) & 3, cols & 31
        source = (s4 << 7) + (((x + k) & 3) << 5) + r
        perm_ref[...] = jnp.where(rows == source, 1.0, 0.0).astype(BF16)

    top, bottom = slice(0, SEG_LEN), slice(SEG_LEN, 2 * SEG_LEN)
    for half in range(2):
        lanes = slice(half * 128, (half + 1) * 128)
        for in_ref, rows, one1, one3 in (
            (h_ref, top, own1, own3),
            (theirs_ref, bottom, theirs1, theirs3),
        ):
            tiles = [
                in_ref[:, pl.ds(pl.multiple_of((half * 4 + s4) * 256 + core * 128, 128), 128)]
                for s4 in range(4)
            ]
            moved = jnp.dot(
                jnp.concatenate(tiles, axis=1), perm_ref[...], preferred_element_type=F32
            ).astype(BF16)
            both0[rows, lanes] = moved[:, 0:128]
            one1[:, lanes] = moved[:, 128:256]
            both2[rows, lanes] = moved[:, 256:384]
            one3[:, lanes] = moved[:, 384:512]


def shuffle(tokens, theirs, where):
    both = jax.ShapeDtypeStruct((2 * SEG_LEN, PART), BF16)
    one = jax.ShapeDtypeStruct((SEG_LEN, PART), BF16)
    both_spec = pl.BlockSpec((2 * SEG_LEN, 256), lambda g, where_ref: (0, (g - where_ref[2]) & 3))
    one_spec = pl.BlockSpec((SEG_LEN, 256), lambda g, where_ref: (0, (g - where_ref[2]) & 3))
    raw = pl.BlockSpec((SEG_LEN, 2048), lambda g, where_ref: (0, g))
    return pl.pallas_call(
        shuffle_kernel,
        grid_spec=pltpu.PrefetchScalarGridSpec(
            num_scalar_prefetch=1,
            grid=(D // 2048,),
            in_specs=[raw, raw],
            out_specs=[both_spec, one_spec, one_spec] * 2,
            scratch_shapes=[pltpu.VMEM((512, 512), BF16)],
        ),
        out_shape=[both, one, one] * 2,
        compiler_params=params(VMEM_LITTLE),
        cost_estimate=pl.CostEstimate(
            flops=2 * 2 * SEG_LEN * 512 * 512 * 8, bytes_accessed=12 << 20, transcendentals=0
        ),
    )(where, tokens, theirs)


def row_blocks(refs):
    both0, own1, theirs1, both2, own3, theirs3 = refs
    top, bottom = slice(0, SEG_LEN), slice(SEG_LEN, 2 * SEG_LEN)
    return (
        (both0[top], both0[bottom]),
        (own1[...], theirs1[...]),
        (both2[top], both2[bottom]),
        (own3[...], theirs3[...]),
    )


def column_specs(block=None):
    def index(step):
        return (0, step if block is None else block)

    both_spec = pl.BlockSpec((2 * SEG_LEN, 256), index)
    one_spec = pl.BlockSpec((SEG_LEN, 256), index)
    return [both_spec, one_spec, one_spec] * 2


def project_kernel(where_ref, *refs):
    columns, pieces, (own_ref, their_ref), weight_ref = refs[:6], refs[6:15], refs[15:17], refs[17]
    x, z = where_ref[0], where_ref[3]
    for d, ref in enumerate(pieces[:7]):
        weight_ref[(z + (0, 1, 2, 3, 5, 6, 7)[d]) & 7] = ref[...]
    weight_ref[(z + 4) & 7, 0:2] = pieces[7][...]
    weight_ref[(z + 4) & 7, 2:4] = pieces[8][...]
    own, theirs = 0.0, 0.0
    for k, (own_rows, their_rows) in enumerate(row_blocks(columns)):
        start = pl.multiple_of(((x + k) & 3) * 32, 32)
        weight = jnp.concatenate(
            [weight_ref[n, e, pl.ds(start, 32), :] for e in range(4) for n in range(ZS)], axis=0
        )
        own = own + dot_nn(own_rows, weight)
        theirs = theirs + dot_nn(their_rows, weight)
    own_ref[...] = own
    their_ref[...] = theirs


def project(where, rows, pieces):
    shape = jax.ShapeDtypeStruct((SEG_LEN, 2 * HEAD), F32)
    return pl.pallas_call(
        project_kernel,
        in_specs=[smem()] + [vmem()] * 15,
        out_specs=[vmem()] * 2,
        out_shape=[shape] * 2,
        scratch_shapes=[pltpu.VMEM((ZS, 4, 128, 2 * HEAD), BF16)],
        compiler_params=params(VMEM_LITTLE),
        cost_estimate=pl.CostEstimate(
            flops=2 * 2 * SEG_LEN * D // 2 * 2 * HEAD, bytes_accessed=7 << 20, transcendentals=0
        ),
    )(where, *rows, *pieces)


def stack_kernel(a_ref, b_ref, out_ref):
    total = (a_ref[...] + b_ref[...]).astype(BF16)
    out_ref[0:SEG_LEN] = total[:, :HEAD]
    out_ref[SEG_LEN : 2 * SEG_LEN] = total[:, HEAD:]


def stack(a, b):
    return pl.pallas_call(
        stack_kernel,
        in_specs=[vmem()] * 2,
        out_specs=vmem(),
        out_shape=jax.ShapeDtypeStruct((2 * SEG_LEN, HEAD), BF16),
        compiler_params=params(),
    )(a, b)


def gradient_kernel(*refs):
    columns, diffs, out_ref = refs[:6], refs[6:14], refs[14]
    blocks = [block for pair in row_blocks(columns) for block in pair]
    total = 0.0
    for block, d_ref in zip(blocks, diffs):
        both = jnp.concatenate([d_ref[0:SEG_LEN], d_ref[SEG_LEN : 2 * SEG_LEN]], axis=1)
        total = total + dot_nn(both.T, block)
    out_ref[...] = total.T


def gradient(columns, diffs, block):
    return pl.pallas_call(
        gradient_kernel,
        grid=(1,),
        in_specs=column_specs(block)
        + [pl.BlockSpec((2 * SEG_LEN, HEAD), lambda i: (0, 0))] * LEAVES,
        out_specs=pl.BlockSpec((SEG_LEN, 2 * HEAD), lambda i: (0, 0)),
        out_shape=jax.ShapeDtypeStruct((SEG_LEN, 2 * HEAD), F32),
        compiler_params=params(),
        cost_estimate=pl.CostEstimate(
            flops=2 * LEAVES * SEG_LEN * SEG_LEN * 2 * HEAD, bytes_accessed=3 << 20, transcendentals=0
        ),
    )(*columns, *diffs)


def place_kernel(where_ref, *refs):
    x, core = where_ref[0], where_ref[1]
    for k in range(XS):
        plane = (x - k) & 3
        for n, half in ((k, core), (XS + k, 1 - core)):
            refs[2 * XS][pl.ds(pl.multiple_of((half * 4 + plane) * 32, 32), 32), :] = refs[n][...]


def place(where, same, swapped):
    return pl.pallas_call(
        place_kernel,
        in_specs=[smem()] + [vmem()] * (2 * XS),
        out_specs=vmem(),
        out_shape=jax.ShapeDtypeStruct((SEG_LEN, 2 * HEAD), F32),
        compiler_params=params(),
    )(where, *same, *swapped)


def ancestors_of(parents_ref, seg):
    first = parents_ref[0, seg]
    second = parents_ref[0, first]
    third = parents_ref[0, second]
    return first, second, third


def select_kernel(parents_ref, owners_ref, in_ref, out_ref):
    def step(seg, carry):
        holder = owners_ref[0, seg]
        for k, ancestor in enumerate(ancestors_of(parents_ref, seg)):
            out_ref[holder, k] = in_ref[owners_ref[0, ancestor]]
        return carry

    lax.fori_loop(0, SEGS, step, 0)


def select_chunks(parents, owners, chunks):
    return pl.pallas_call(
        select_kernel,
        in_specs=[smem(), smem(), vmem()],
        out_specs=vmem(),
        out_shape=jax.ShapeDtypeStruct((SEGS, DEPTH - 1, CHUNK, HEAD), BF16),
        compiler_params=params(),
    )(parents, owners, chunks)


def collect_kernel(parents_ref, owners_ref, in_ref, out_ref):
    out_ref[...] = jnp.zeros_like(out_ref)

    def step(seg, carry):
        holder = owners_ref[0, seg]
        for k, ancestor in enumerate(ancestors_of(parents_ref, seg)):
            target = owners_ref[0, ancestor]
            out_ref[target] += in_ref[holder, k].astype(F32)
        return carry

    lax.fori_loop(0, SEGS, step, 0)


def collect_chunks(parents, owners, grads):
    return pl.pallas_call(
        collect_kernel,
        in_specs=[smem(), smem(), vmem()],
        out_specs=vmem(),
        out_shape=jax.ShapeDtypeStruct((SEGS, CHUNK, HEAD), F32),
        compiler_params=params(),
    )(parents, owners, grads)


def dot_nt(a, b):
    return lax.dot_general(a, b, (((1,), (1,)), ((), ())), preferred_element_type=F32)


def dot_nn(a, b):
    return jnp.dot(a, b, preferred_element_type=F32)


def attend_kernel(
    depth_ref, own_ref, anc_ref, q_ref, g_ref,
    out_ref, qgrad_ref, own_grad_ref, anc_grad_ref,
    keys_ref, values_ref, keys_t_ref, values_t_ref, dk_ref, dv_ref,
):
    step = pl.program_id(0)
    factor = HEAD ** (-0.5)
    log2_factor = factor * math.log2(math.e)
    half = SEGS // 2
    blocks = [slice(b * SEG_LEN, (b + 1) * SEG_LEN) for b in range(DEPTH)]

    @pl.when(step == 0)
    def _():
        keys_ref[blocks[0]] = own_ref[0:SEG_LEN]
        values_ref[blocks[0]] = own_ref[SEG_LEN : 2 * SEG_LEN]
        for b in range(1, DEPTH):
            keys_ref[blocks[b]] = anc_ref[0:half, b - 1].reshape(SEG_LEN, HEAD)
            values_ref[blocks[b]] = anc_ref[half:SEGS, b - 1].reshape(SEG_LEN, HEAD)
        keys_t_ref[...] = keys_ref[...].T
        values_t_ref[...] = values_ref[...].T
        dk_ref[...] = jnp.zeros_like(dk_ref)
        dv_ref[...] = jnp.zeros_like(dv_ref)

    depth = depth_ref[0]
    causal = lax.broadcasted_iota(jnp.int32, (SEG_LEN, SEG_LEN), 0) <= lax.broadcasted_iota(
        jnp.int32, (SEG_LEN, SEG_LEN), 1
    )
    for h in range(STEP_HEADS):
        cols = slice(h * HEAD, (h + 1) * HEAD)
        q = q_ref[:, cols]
        g = g_ref[:, cols]
        scores = []
        for b in range(DEPTH):
            block = dot_nt(keys_ref[blocks[b]], q)
            if b == 0:
                block = jnp.where(causal, block, -jnp.inf)
            else:
                block = block + jnp.where(depth >= b, 0.0, -jnp.inf)
            scores.append(block)
        peak = jnp.max(functools.reduce(jnp.maximum, scores), axis=0, keepdims=True) * log2_factor
        expd = [jnp.exp2(block * log2_factor - peak) for block in scores]
        scale = 1.0 / sum(jnp.sum(block, axis=0, keepdims=True) for block in expd)
        probs = [(block * scale).astype(BF16) for block in expd]
        dprobs = [dot_nt(values_ref[blocks[b]], g) for b in range(DEPTH)]
        centre = sum(
            jnp.sum(p.astype(F32) * dp, axis=0, keepdims=True) for p, dp in zip(probs, dprobs)
        )
        dscores = [(p.astype(F32) * (dp - centre)).astype(BF16) for p, dp in zip(probs, dprobs)]
        probs = jnp.concatenate(probs, axis=0)
        dscores = jnp.concatenate(dscores, axis=0)
        out_ref[:, cols] = dot_nn(values_t_ref[...], probs).T.astype(BF16)
        qgrad_ref[:, cols] = (dot_nn(keys_t_ref[...], dscores).T * factor).astype(BF16)
        dk_ref[...] += dot_nn(dscores, q)
        dv_ref[...] += dot_nn(probs, g)

    @pl.when(step == HEADS // STEP_HEADS - 1)
    def _():
        own_grad_ref[0:SEG_LEN] = dk_ref[blocks[0]] * factor
        own_grad_ref[SEG_LEN : 2 * SEG_LEN] = dv_ref[blocks[0]]
        for b in range(1, DEPTH):
            anc_grad_ref[0:half, b - 1] = (
                (dk_ref[blocks[b]] * factor).astype(BF16).reshape(half, CHUNK, HEAD)
            )
            anc_grad_ref[half:SEGS, b - 1] = (
                dv_ref[blocks[b]].astype(BF16).reshape(half, CHUNK, HEAD)
            )


def attend(depth, own, anc, queries, grads):
    head = pl.BlockSpec((SEG_LEN, STEP_HEADS * HEAD), lambda h: (0, h))
    keys = DEPTH * SEG_LEN
    return pl.pallas_call(
        attend_kernel,
        grid=(HEADS // STEP_HEADS,),
        in_specs=[
            smem(),
            pl.BlockSpec((2 * SEG_LEN, HEAD), lambda h: (0, 0)),
            pl.BlockSpec((SEGS, DEPTH - 1, CHUNK, HEAD), lambda h: (0, 0, 0, 0)),
            head,
            head,
        ],
        out_specs=[
            head,
            head,
            pl.BlockSpec((2 * SEG_LEN, HEAD), lambda h: (0, 0)),
            pl.BlockSpec((SEGS, DEPTH - 1, CHUNK, HEAD), lambda h: (0, 0, 0, 0)),
        ],
        out_shape=[
            jax.ShapeDtypeStruct((SEG_LEN, HEADS * HEAD), BF16),
            jax.ShapeDtypeStruct((SEG_LEN, HEADS * HEAD), BF16),
            jax.ShapeDtypeStruct((2 * SEG_LEN, HEAD), F32),
            jax.ShapeDtypeStruct((SEGS, DEPTH - 1, CHUNK, HEAD), BF16),
        ],
        scratch_shapes=[
            pltpu.VMEM((keys, HEAD), BF16),
            pltpu.VMEM((keys, HEAD), BF16),
            pltpu.VMEM((HEAD, keys), BF16),
            pltpu.VMEM((HEAD, keys), BF16),
            pltpu.VMEM((keys, HEAD), F32),
            pltpu.VMEM((keys, HEAD), F32),
        ],
        compiler_params=params(VMEM_MOST),
        cost_estimate=pl.CostEstimate(
            flops=0, bytes_accessed=0, transcendentals=0
        ),
    )(depth, own, anc, queries, grads)


def x_shift(value, steps, flip=0):
    pairs = [(i, ((i + 2 * steps) % LEAVES) ^ flip) for i in range(LEAVES)]
    return lax.ppermute(value, "leaf", pairs)


def core_swap(value):
    return x_shift(value, 0, 1)


def y_shift(value, steps):
    return lax.ppermute(value, "seg", [(i, (i + ZS * steps) % SEGS) for i in range(SEGS)])


def z_shift(value, steps):
    pairs = [(i, i // ZS * ZS + (i + steps) % ZS) for i in range(SEGS)]
    return lax.ppermute(value, "seg", pairs)


def over_z(value):
    groups = [list(range(i, i + ZS)) for i in range(0, SEGS, ZS)]
    return lax.all_to_all(value, "seg", 0, 0, axis_index_groups=groups, tiled=True)


def over_seg(value):
    return lax.all_to_all(value, "seg", 0, 0, tiled=True)


def per_device(hidden_states, queries, key_value_weight, attention_grad, parents, owners, depths):
    leaf = lax.axis_index("leaf")
    position = lax.axis_index("seg")
    x, core, y = leaf // 2, leaf % 2, position // ZS
    where = jnp.stack([x, core, y, position % ZS]).astype(jnp.int32)
    depth = jnp.sum(jnp.where(owners[0] == position, depths[0], 0)).reshape(1)

    tokens = hidden_states[0]
    half = lax.dynamic_slice_in_dim(key_value_weight, core * 128, 128, 0)
    piece = jnp.stack([half] + [y_shift(half, -e) for e in range(1, 4)])
    piece, theirs = lax.optimization_barrier((piece, core_swap(tokens)))
    ahead1, behind1 = z_shift(piece, -1), z_shift(piece, 1)
    ahead1, behind1, rows = lax.optimization_barrier(
        (ahead1, behind1, shuffle(tokens, theirs, where))
    )
    ahead2, behind2 = z_shift(ahead1, -1), z_shift(behind1, 1)
    ahead3, behind3 = z_shift(ahead2, -1), z_shift(behind2, 1)

    columns = list(rows)
    columns[1], columns[4] = x_shift(rows[1], 1), x_shift(rows[4], 3)
    ahead3, behind3, columns = lax.optimization_barrier((ahead3, behind3, columns))
    opposite = z_shift(ahead3[:2], -1), z_shift(behind3[2:], 1)
    pieces = (piece, ahead1, ahead2, ahead3, behind3, behind2, behind1, *opposite)
    own_part, their_part = project(where, rows, pieces)
    columns[2], columns[5] = x_shift(rows[2], 1), x_shift(rows[5], 3)
    stacked = stack(own_part, core_swap(their_part))

    def settle(value, *places):
        value, got = lax.optimization_barrier((value, [columns[n] for n in places]))
        for n, block in zip(places, got):
            columns[n] = block
        return value

    chunks = settle(over_seg(stacked.reshape(SEGS, CHUNK, HEAD)), 2, 5)
    chunks, both2 = lax.optimization_barrier((chunks, rows[3]))
    columns[3] = x_shift(both2, 2)
    ancestors = over_seg(select_chunks(parents, owners, chunks))
    output, query_grad, own_grad, anc_grad = attend(
        depth, stacked, ancestors, queries[0], attention_grad[0]
    )
    arrived = over_seg(settle(anc_grad, 3))
    returned = over_seg(collect_chunks(parents, owners, arrived))
    diff = (own_grad + returned.reshape(2 * SEG_LEN, HEAD)).astype(BF16)

    diffs = [diff] + [x_shift(diff, k) for k in range(1, XS)]
    swapped = [core_swap(d) for d in diffs]
    pairs = [d for k in range(XS) for d in (diffs[k], swapped[k])]
    blocks = {e: gradient(columns, pairs, e) for e in (2, 1, 3, 0)}
    summed = blocks[0]
    for e in (1, 3, 2):
        summed = summed + y_shift(blocks[e], e)
    factor = float(LEAVES * SEGS * SEG_LEN) ** (-0.5)
    share = jnp.sum(over_z(summed.reshape(ZS, 32, 2 * HEAD)), axis=0) * factor
    shares = [share] + [x_shift(share, k) for k in range(1, XS)]
    grad_block = place(where, shares, [core_swap(s) for s in shares])
    return (output[None], query_grad[None], grad_block)


def solution(mesh):
    placed = (
        P("leaf", "seg", None),
        P("leaf", "seg", None),
        P("seg", None),
        P("leaf", "seg", None),
        P("leaf", None),
        P("leaf", None),
        P("leaf", None),
    )
    return jax.shard_map(
        per_device,
        mesh=mesh,
        in_specs=placed,
        out_specs=(P("leaf", "seg", None), P("leaf", "seg", None), P("seg", None)),
        check_vma=False,
    )
```

```python
import functools
import math

import jax
import jax.numpy as jnp
from jax import lax
from jax.experimental import pallas as pl
from jax.experimental.pallas import tpu as pltpu
from jax.sharding import PartitionSpec as P

HEAD = 128
HEADS = 8
DEPTH = 4
SEGS = 32
SEG_LEN = 256
LEAVES = 8
D = 8192
XS = 4
ZS = 8
STEP_HEADS = 2
CHUNK = 2 * SEG_LEN // SEGS
PART = D // LEAVES
F32 = jnp.float32
BF16 = jnp.bfloat16
VMEM_LIMIT = 40 * 1024 * 1024
VMEM_MOST = 60 * 1024 * 1024
VMEM_LITTLE = 16 * 1024 * 1024


def smem():
    return pl.BlockSpec(memory_space=pltpu.SMEM)


def vmem():
    return pl.BlockSpec(memory_space=pltpu.VMEM)


def params(limit=VMEM_LIMIT):
    return pltpu.CompilerParams(vmem_limit_bytes=limit)


def shuffle_kernel(planes, where_ref, own_ref, theirs_ref, out0_ref, out1_ref, perm_ref):
    x, core, y = where_ref[0], where_ref[1], where_ref[2]
    count = own_ref.shape[0]

    @pl.when(pl.program_id(0) == 0)
    def _():
        rows = lax.broadcasted_iota(jnp.int32, (512, 256), 0)
        cols = lax.broadcasted_iota(jnp.int32, (512, 256), 1)
        k = jnp.where(cols < 128, planes[0], planes[1])
        s4, r = (cols >> 5) & 3, cols & 31
        source = (s4 << 7) + (((x + k) & 3) << 5) + r
        perm_ref[...] = jnp.where(rows == source, 1.0, 0.0).astype(BF16)

    for g in range(8):
        lanes = pl.ds(pl.multiple_of(((g // 2 - y) & 3) * 256 + g % 2 * 128, 128), 128)
        tiles = [
            jnp.concatenate(
                [
                    ref[:, pl.ds(pl.multiple_of((4 * g + s4) * 256 + core * 128, 128), 128)]
                    for s4 in range(4)
                ],
                axis=1,
            )
            for ref in (own_ref, theirs_ref)
        ]
        moved = jnp.dot(
            jnp.concatenate(tiles, axis=0), perm_ref[...], preferred_element_type=F32
        ).astype(BF16)
        for n in range(2):
            out0_ref[n, :, lanes] = moved[n * count : (n + 1) * count, 0:128]
            out1_ref[n, :, lanes] = moved[n * count : (n + 1) * count, 128:256]


def shuffle(tokens, theirs, where, planes):
    step = SEG_LEN // 2
    raw = pl.BlockSpec((step, D), lambda i: (i, 0))
    out = pl.pallas_call(
        functools.partial(shuffle_kernel, planes),
        grid=(2,),
        in_specs=[smem(), raw, raw],
        out_specs=[pl.BlockSpec((2, step, PART), lambda i: (0, i, 0))] * 2,
        out_shape=[jax.ShapeDtypeStruct((2, SEG_LEN, PART), BF16)] * 2,
        scratch_shapes=[pltpu.VMEM((512, 256), BF16)],
        compiler_params=params(VMEM_MOST),
        cost_estimate=pl.CostEstimate(
            flops=2 * 2 * SEG_LEN * 512 * 256 * 8, bytes_accessed=10 << 20, transcendentals=0
        ),
    )(where, tokens, theirs)
    return [block.reshape(2 * SEG_LEN, PART) for block in out]


def project_kernel(where_ref, own_ref, theirs_ref, *refs):
    pieces, outs = refs[:16], refs[16:]
    core, y, z = where_ref[1], where_ref[2], where_ref[3]
    for rows_ref, out_ref in ((own_ref, outs[0]), (theirs_ref, outs[1])):
        total = 0.0
        for n, ref in enumerate(pieces):
            tiles = []
            for e in (2 * (n // 8), 2 * (n // 8) + 1):
                shard = ((y + e) & 3) * ZS + ((z + n % 8) & 7)
                start = pl.multiple_of(shard * 256 + core * 128, 128)
                tiles.append(rows_ref[:, pl.ds(start, 128)])
            total = total + dot_nn(jnp.concatenate(tiles, axis=1), ref[...])
        out_ref[...] = total


def project(where, tokens, theirs, pieces):
    shape = jax.ShapeDtypeStruct((SEG_LEN, 2 * HEAD), F32)
    return pl.pallas_call(
        project_kernel,
        in_specs=[smem()] + [vmem()] * 18,
        out_specs=[vmem()] * 2,
        out_shape=[shape] * 2,
        compiler_params=params(VMEM_LITTLE),
        cost_estimate=pl.CostEstimate(
            flops=2 * 2 * SEG_LEN * D // 2 * 2 * HEAD, bytes_accessed=7 << 20, transcendentals=0
        ),
    )(where, tokens, theirs, *pieces)


def stack_kernel(a_ref, b_ref, out_ref):
    total = (a_ref[...] + b_ref[...]).astype(BF16)
    out_ref[0:SEG_LEN] = total[:, :HEAD]
    out_ref[SEG_LEN : 2 * SEG_LEN] = total[:, HEAD:]


def stack(a, b):
    return pl.pallas_call(
        stack_kernel,
        in_specs=[vmem()] * 2,
        out_specs=vmem(),
        out_shape=jax.ShapeDtypeStruct((2 * SEG_LEN, HEAD), BF16),
        compiler_params=params(),
    )(a, b)


def gradient_kernel(*refs):
    columns, diffs, out_ref = refs[:4], refs[4:12], refs[12]
    total = 0.0
    for k in range(XS):
        for n in range(2):
            d_ref = diffs[2 * k + n]
            both = jnp.concatenate([d_ref[0:SEG_LEN], d_ref[SEG_LEN : 2 * SEG_LEN]], axis=1)
            total = total + dot_nn(both.T, columns[k][n * SEG_LEN : (n + 1) * SEG_LEN])
    out_ref[...] = total.T


def gradient(columns, diffs, block):
    return pl.pallas_call(
        gradient_kernel,
        grid=(1,),
        in_specs=[pl.BlockSpec((2 * SEG_LEN, SEG_LEN), lambda i: (0, block))] * XS
        + [pl.BlockSpec((2 * SEG_LEN, HEAD), lambda i: (0, 0))] * LEAVES,
        out_specs=pl.BlockSpec((SEG_LEN, 2 * HEAD), lambda i: (0, 0)),
        out_shape=jax.ShapeDtypeStruct((SEG_LEN, 2 * HEAD), F32),
        compiler_params=params(),
        cost_estimate=pl.CostEstimate(
            flops=2 * LEAVES * SEG_LEN * SEG_LEN * 2 * HEAD, bytes_accessed=3 << 20, transcendentals=0
        ),
    )(*columns, *diffs)


def place_kernel(where_ref, *refs):
    x, core = where_ref[0], where_ref[1]
    for k in range(XS):
        plane = (x - k) & 3
        for n, half in ((k, core), (XS + k, 1 - core)):
            refs[2 * XS][pl.ds(pl.multiple_of((half * 4 + plane) * 32, 32), 32), :] = refs[n][...]


def place(where, same, swapped):
    return pl.pallas_call(
        place_kernel,
        in_specs=[smem()] + [vmem()] * (2 * XS),
        out_specs=vmem(),
        out_shape=jax.ShapeDtypeStruct((SEG_LEN, 2 * HEAD), F32),
        compiler_params=params(),
    )(where, *same, *swapped)


def ancestors_of(parents_ref, seg):
    first = parents_ref[0, seg]
    second = parents_ref[0, first]
    third = parents_ref[0, second]
    return first, second, third


def select_kernel(parents_ref, owners_ref, in_ref, out_ref):
    def step(seg, carry):
        holder = owners_ref[0, seg]
        for k, ancestor in enumerate(ancestors_of(parents_ref, seg)):
            out_ref[holder, k] = in_ref[owners_ref[0, ancestor]]
        return carry

    lax.fori_loop(0, SEGS, step, 0)


def select_chunks(parents, owners, chunks):
    return pl.pallas_call(
        select_kernel,
        in_specs=[smem(), smem(), vmem()],
        out_specs=vmem(),
        out_shape=jax.ShapeDtypeStruct((SEGS, DEPTH - 1, CHUNK, HEAD), BF16),
        compiler_params=params(),
    )(parents, owners, chunks)


def collect_kernel(parents_ref, owners_ref, in_ref, out_ref):
    out_ref[...] = jnp.zeros_like(out_ref)

    def step(seg, carry):
        holder = owners_ref[0, seg]
        for k, ancestor in enumerate(ancestors_of(parents_ref, seg)):
            target = owners_ref[0, ancestor]
            out_ref[target] += in_ref[holder, k].astype(F32)
        return carry

    lax.fori_loop(0, SEGS, step, 0)


def collect_chunks(parents, owners, grads):
    return pl.pallas_call(
        collect_kernel,
        in_specs=[smem(), smem(), vmem()],
        out_specs=vmem(),
        out_shape=jax.ShapeDtypeStruct((SEGS, CHUNK, HEAD), F32),
        compiler_params=params(),
    )(parents, owners, grads)


def dot_nt(a, b):
    return lax.dot_general(a, b, (((1,), (1,)), ((), ())), preferred_element_type=F32)


def dot_nn(a, b):
    return jnp.dot(a, b, preferred_element_type=F32)


def attend_kernel(
    depth_ref, own_ref, anc_ref, q_ref, g_ref,
    out_ref, qgrad_ref, own_grad_ref, anc_grad_ref,
    keys_ref, values_ref, keys_t_ref, values_t_ref, dk_ref, dv_ref,
):
    step = pl.program_id(0)
    factor = HEAD ** (-0.5)
    log2_factor = factor * math.log2(math.e)
    half = SEGS // 2
    blocks = [slice(b * SEG_LEN, (b + 1) * SEG_LEN) for b in range(DEPTH)]

    @pl.when(step == 0)
    def _():
        keys_ref[blocks[0]] = own_ref[0:SEG_LEN]
        values_ref[blocks[0]] = own_ref[SEG_LEN : 2 * SEG_LEN]
        for b in range(1, DEPTH):
            keys_ref[blocks[b]] = anc_ref[0:half, b - 1].reshape(SEG_LEN, HEAD)
            values_ref[blocks[b]] = anc_ref[half:SEGS, b - 1].reshape(SEG_LEN, HEAD)
        keys_t_ref[...] = keys_ref[...].T
        values_t_ref[...] = values_ref[...].T
        dk_ref[...] = jnp.zeros_like(dk_ref)
        dv_ref[...] = jnp.zeros_like(dv_ref)

    depth = depth_ref[0]
    causal = lax.broadcasted_iota(jnp.int32, (SEG_LEN, SEG_LEN), 0) <= lax.broadcasted_iota(
        jnp.int32, (SEG_LEN, SEG_LEN), 1
    )
    for h in range(STEP_HEADS):
        cols = slice(h * HEAD, (h + 1) * HEAD)
        q = q_ref[:, cols]
        g = g_ref[:, cols]
        scores = []
        for b in range(DEPTH):
            block = dot_nt(keys_ref[blocks[b]], q)
            if b == 0:
                block = jnp.where(causal, block, -jnp.inf)
            else:
                block = block + jnp.where(depth >= b, 0.0, -jnp.inf)
            scores.append(block)
        peak = jnp.max(functools.reduce(jnp.maximum, scores), axis=0, keepdims=True) * log2_factor
        expd = [jnp.exp2(block * log2_factor - peak) for block in scores]
        scale = 1.0 / sum(jnp.sum(block, axis=0, keepdims=True) for block in expd)
        probs = [(block * scale).astype(BF16) for block in expd]
        dprobs = [dot_nt(values_ref[blocks[b]], g) for b in range(DEPTH)]
        centre = sum(
            jnp.sum(p.astype(F32) * dp, axis=0, keepdims=True) for p, dp in zip(probs, dprobs)
        )
        dscores = [(p.astype(F32) * (dp - centre)).astype(BF16) for p, dp in zip(probs, dprobs)]
        probs = jnp.concatenate(probs, axis=0)
        dscores = jnp.concatenate(dscores, axis=0)
        out_ref[:, cols] = dot_nn(values_t_ref[...], probs).T.astype(BF16)
        qgrad_ref[:, cols] = (dot_nn(keys_t_ref[...], dscores).T * factor).astype(BF16)
        dk_ref[...] += dot_nn(dscores, q)
        dv_ref[...] += dot_nn(probs, g)

    @pl.when(step == HEADS // STEP_HEADS - 1)
    def _():
        own_grad_ref[0:SEG_LEN] = dk_ref[blocks[0]] * factor
        own_grad_ref[SEG_LEN : 2 * SEG_LEN] = dv_ref[blocks[0]]
        for b in range(1, DEPTH):
            anc_grad_ref[0:half, b - 1] = (
                (dk_ref[blocks[b]] * factor).astype(BF16).reshape(half, CHUNK, HEAD)
            )
            anc_grad_ref[half:SEGS, b - 1] = (
                dv_ref[blocks[b]].astype(BF16).reshape(half, CHUNK, HEAD)
            )


def attend(depth, own, anc, queries, grads):
    head = pl.BlockSpec((SEG_LEN, STEP_HEADS * HEAD), lambda h: (0, h))
    keys = DEPTH * SEG_LEN
    return pl.pallas_call(
        attend_kernel,
        grid=(HEADS // STEP_HEADS,),
        in_specs=[
            smem(),
            pl.BlockSpec((2 * SEG_LEN, HEAD), lambda h: (0, 0)),
            pl.BlockSpec((SEGS, DEPTH - 1, CHUNK, HEAD), lambda h: (0, 0, 0, 0)),
            head,
            head,
        ],
        out_specs=[
            head,
            head,
            pl.BlockSpec((2 * SEG_LEN, HEAD), lambda h: (0, 0)),
            pl.BlockSpec((SEGS, DEPTH - 1, CHUNK, HEAD), lambda h: (0, 0, 0, 0)),
        ],
        out_shape=[
            jax.ShapeDtypeStruct((SEG_LEN, HEADS * HEAD), BF16),
            jax.ShapeDtypeStruct((SEG_LEN, HEADS * HEAD), BF16),
            jax.ShapeDtypeStruct((2 * SEG_LEN, HEAD), F32),
            jax.ShapeDtypeStruct((SEGS, DEPTH - 1, CHUNK, HEAD), BF16),
        ],
        scratch_shapes=[
            pltpu.VMEM((keys, HEAD), BF16),
            pltpu.VMEM((keys, HEAD), BF16),
            pltpu.VMEM((HEAD, keys), BF16),
            pltpu.VMEM((HEAD, keys), BF16),
            pltpu.VMEM((keys, HEAD), F32),
            pltpu.VMEM((keys, HEAD), F32),
        ],
        compiler_params=params(VMEM_MOST),
        cost_estimate=pl.CostEstimate(
            flops=0, bytes_accessed=0, transcendentals=0
        ),
    )(depth, own, anc, queries, grads)


def x_shift(value, steps, flip=0):
    pairs = [(i, ((i + 2 * steps) % LEAVES) ^ flip) for i in range(LEAVES)]
    return lax.ppermute(value, "leaf", pairs)


def core_swap(value):
    return x_shift(value, 0, 1)


def y_shift(value, steps):
    return lax.ppermute(value, "seg", [(i, (i + ZS * steps) % SEGS) for i in range(SEGS)])


def z_shift(value, steps):
    pairs = [(i, i // ZS * ZS + (i + steps) % ZS) for i in range(SEGS)]
    return lax.ppermute(value, "seg", pairs)


def over_z(value):
    groups = [list(range(i, i + ZS)) for i in range(0, SEGS, ZS)]
    return lax.all_to_all(value, "seg", 0, 0, axis_index_groups=groups, tiled=True)


def over_seg(value):
    return lax.all_to_all(value, "seg", 0, 0, tiled=True)


def per_device(hidden_states, queries, key_value_weight, attention_grad, parents, owners, depths):
    leaf = lax.axis_index("leaf")
    position = lax.axis_index("seg")
    x, core, y = leaf // 2, leaf % 2, position // ZS
    where = jnp.stack([x, core, y, position % ZS]).astype(jnp.int32)
    depth = jnp.sum(jnp.where(owners[0] == position, depths[0], 0)).reshape(1)

    tokens = hidden_states[0]
    half = lax.dynamic_slice_in_dim(key_value_weight, core * 128, 128, 0)
    theirs = core_swap(tokens)
    near = jnp.concatenate([half, y_shift(half, -1)])
    far = jnp.concatenate([y_shift(half, -2), y_shift(half, -3)])
    pieces = []
    for first, way in ((near, -1), (far, 1)):
        ring = {0: first}
        for d in range(1, 4):
            ring[d] = z_shift(ring[d - 1], -1)
            ring[8 - d] = z_shift(ring[(9 - d) % 8], 1)
        ring[4] = z_shift(ring[4 + way], way)
        pieces.extend(ring[d] for d in range(8))
    own_part, their_part = project(where, tokens, theirs, pieces)
    stacked = stack(own_part, core_swap(their_part))

    stacked, theirs = lax.optimization_barrier((stacked, theirs))
    both1, both3 = shuffle(tokens, theirs, where, (1, 3))
    chunks = over_seg(stacked.reshape(SEGS, CHUNK, HEAD))
    chunks, both1, both3, theirs = lax.optimization_barrier((chunks, both1, both3, theirs))
    moved1, moved3 = x_shift(both1, 1), x_shift(both3, 3)
    both0, both2 = shuffle(tokens, theirs, where, (0, 2))
    ancestors = over_seg(select_chunks(parents, owners, chunks))
    ancestors, both0, both2 = lax.optimization_barrier((ancestors, both0, both2))
    output, query_grad, own_grad, anc_grad = attend(
        depth, stacked, ancestors, queries[0], attention_grad[0]
    )
    anc_grad, moved1, moved3, both2 = lax.optimization_barrier((anc_grad, moved1, moved3, both2))
    moved2 = x_shift(both2, 2)
    arrived = over_seg(anc_grad)
    returned = over_seg(collect_chunks(parents, owners, arrived))
    returned, moved2 = lax.optimization_barrier((returned, moved2))
    diff = (own_grad + returned.reshape(2 * SEG_LEN, HEAD)).astype(BF16)

    diffs = [diff] + [x_shift(diff, k) for k in range(1, XS)]
    swapped = [core_swap(d) for d in diffs]
    pairs = [d for k in range(XS) for d in (diffs[k], swapped[k])]
    columns = (both0, moved1, moved2, moved3)
    blocks = {e: gradient(columns, pairs, e) for e in (2, 1, 3, 0)}
    summed = blocks[0]
    for e in (1, 3, 2):
        summed = summed + y_shift(blocks[e], e)
    factor = float(LEAVES * SEGS * SEG_LEN) ** (-0.5)
    share = jnp.sum(over_z(summed.reshape(ZS, 32, 2 * HEAD)), axis=0) * factor
    shares = [share] + [x_shift(share, k) for k in range(1, XS)]
    grad_block = place(where, shares, [core_swap(s) for s in shares])
    return (output[None], query_grad[None], grad_block)


def solution(mesh):
    placed = (
        P("leaf", "seg", None),
        P("leaf", "seg", None),
        P("seg", None),
        P("leaf", "seg", None),
        P("leaf", None),
        P("leaf", None),
        P("leaf", None),
    )
    return jax.shard_map(
        per_device,
        mesh=mesh,
        in_specs=placed,
        out_specs=(P("leaf", "seg", None), P("leaf", "seg", None), P("seg", None)),
        check_vma=False,
    )
```

```python
import functools
import math

import jax
import jax.numpy as jnp
from jax import lax
from jax.experimental import pallas as pl
from jax.experimental.pallas import tpu as pltpu
from jax.sharding import PartitionSpec as P

HEAD = 128
HEADS = 8
DEPTH = 4
SEGS = 32
SEG_LEN = 256
LEAVES = 8
D = 8192
XS = 4
ZS = 8
STEP_HEADS = 2
CHUNK = 2 * SEG_LEN // SEGS
PART = D // LEAVES
F32 = jnp.float32
BF16 = jnp.bfloat16
VMEM_LIMIT = 40 * 1024 * 1024
VMEM_MOST = 60 * 1024 * 1024
VMEM_LITTLE = 16 * 1024 * 1024


def smem():
    return pl.BlockSpec(memory_space=pltpu.SMEM)


def vmem():
    return pl.BlockSpec(memory_space=pltpu.VMEM)


def params(limit=VMEM_LIMIT):
    return pltpu.CompilerParams(vmem_limit_bytes=limit)


def shuffle_kernel(planes, where_ref, own_ref, theirs_ref, out0_ref, out1_ref, perm_ref):
    x, core, y = where_ref[0], where_ref[1], where_ref[2]
    count = own_ref.shape[0]

    @pl.when(pl.program_id(0) == 0)
    def _():
        rows = lax.broadcasted_iota(jnp.int32, (512, 256), 0)
        cols = lax.broadcasted_iota(jnp.int32, (512, 256), 1)
        k = jnp.where(cols < 128, planes[0], planes[1])
        s4, r = (cols >> 5) & 3, cols & 31
        source = (s4 << 7) + (((x + k) & 3) << 5) + r
        perm_ref[...] = jnp.where(rows == source, 1.0, 0.0).astype(BF16)

    def group(g, carry):
        lanes = pl.ds(pl.multiple_of((((g >> 1) - y) & 3) * 256 + (g & 1) * 128, 128), 128)
        tiles = [
            jnp.concatenate(
                [
                    ref[:, pl.ds(pl.multiple_of((4 * g + s4) * 256 + core * 128, 128), 128)]
                    for s4 in range(4)
                ],
                axis=1,
            )
            for ref in (own_ref, theirs_ref)
        ]
        moved = jnp.dot(
            jnp.concatenate(tiles, axis=0), perm_ref[...], preferred_element_type=F32
        ).astype(BF16)
        for n in range(2):
            out0_ref[n, :, lanes] = moved[n * count : (n + 1) * count, 0:128]
            out1_ref[n, :, lanes] = moved[n * count : (n + 1) * count, 128:256]
        return carry

    lax.fori_loop(0, 8, group, 0, unroll=2)


def shuffle(tokens, theirs, where, planes):
    step = SEG_LEN // 2
    raw = pl.BlockSpec((step, D), lambda i: (i, 0))
    out = pl.pallas_call(
        functools.partial(shuffle_kernel, planes),
        grid=(2,),
        in_specs=[smem(), raw, raw],
        out_specs=[pl.BlockSpec((2, step, PART), lambda i: (0, i, 0))] * 2,
        out_shape=[jax.ShapeDtypeStruct((2, SEG_LEN, PART), BF16)] * 2,
        scratch_shapes=[pltpu.VMEM((512, 256), BF16)],
        compiler_params=params(VMEM_MOST),
        cost_estimate=pl.CostEstimate(
            flops=2 * 2 * SEG_LEN * 512 * 256 * 8, bytes_accessed=10 << 20, transcendentals=0
        ),
    )(where, tokens, theirs)
    return [block.reshape(2 * SEG_LEN, PART) for block in out]


def project_kernel(where_ref, own_ref, theirs_ref, *refs):
    pieces, outs = refs[:16], refs[16:]
    core, y, z = where_ref[1], where_ref[2], where_ref[3]
    for rows_ref, out_ref in ((own_ref, outs[0]), (theirs_ref, outs[1])):
        total = 0.0
        for n, ref in enumerate(pieces):
            tiles = []
            for e in (2 * (n // 8), 2 * (n // 8) + 1):
                shard = ((y + e) & 3) * ZS + ((z + n % 8) & 7)
                start = pl.multiple_of(shard * 256 + core * 128, 128)
                tiles.append(rows_ref[:, pl.ds(start, 128)])
            total = total + dot_nn(jnp.concatenate(tiles, axis=1), ref[...])
        out_ref[...] = total


def project(where, tokens, theirs, pieces):
    shape = jax.ShapeDtypeStruct((SEG_LEN, 2 * HEAD), F32)
    return pl.pallas_call(
        project_kernel,
        in_specs=[smem()] + [vmem()] * 18,
        out_specs=[vmem()] * 2,
        out_shape=[shape] * 2,
        compiler_params=params(VMEM_LITTLE),
        cost_estimate=pl.CostEstimate(
            flops=2 * 2 * SEG_LEN * D // 2 * 2 * HEAD, bytes_accessed=7 << 20, transcendentals=0
        ),
    )(where, tokens, theirs, *pieces)


def stack_kernel(a_ref, b_ref, out_ref):
    total = (a_ref[...] + b_ref[...]).astype(BF16)
    out_ref[0:SEG_LEN] = total[:, :HEAD]
    out_ref[SEG_LEN : 2 * SEG_LEN] = total[:, HEAD:]


def stack(a, b):
    return pl.pallas_call(
        stack_kernel,
        in_specs=[vmem()] * 2,
        out_specs=vmem(),
        out_shape=jax.ShapeDtypeStruct((2 * SEG_LEN, HEAD), BF16),
        compiler_params=params(),
    )(a, b)


def gradient_kernel(*refs):
    columns, diffs, out_ref = refs[:4], refs[4:12], refs[12]
    total = 0.0
    for k in range(XS):
        for n in range(2):
            d_ref = diffs[2 * k + n]
            both = jnp.concatenate([d_ref[0:SEG_LEN], d_ref[SEG_LEN : 2 * SEG_LEN]], axis=1)
            total = total + dot_nn(both.T, columns[k][n * SEG_LEN : (n + 1) * SEG_LEN])
    out_ref[...] = total.T


def gradient(columns, diffs, block):
    return pl.pallas_call(
        gradient_kernel,
        grid=(1,),
        in_specs=[pl.BlockSpec((2 * SEG_LEN, SEG_LEN), lambda i: (0, block))] * XS
        + [pl.BlockSpec((2 * SEG_LEN, HEAD), lambda i: (0, 0))] * LEAVES,
        out_specs=pl.BlockSpec((SEG_LEN, 2 * HEAD), lambda i: (0, 0)),
        out_shape=jax.ShapeDtypeStruct((SEG_LEN, 2 * HEAD), F32),
        compiler_params=params(),
        cost_estimate=pl.CostEstimate(
            flops=2 * LEAVES * SEG_LEN * SEG_LEN * 2 * HEAD, bytes_accessed=3 << 20, transcendentals=0
        ),
    )(*columns, *diffs)


def pair_kernel(where_ref, mine_ref, other_ref, out_ref):
    core = where_ref[1]
    out_ref[pl.ds(pl.multiple_of(core * 32, 32), 32), :] = mine_ref[...]
    out_ref[pl.ds(pl.multiple_of((1 - core) * 32, 32), 32), :] = other_ref[...]


def pair_up(where, mine, other):
    return pl.pallas_call(
        pair_kernel,
        in_specs=[smem(), vmem(), vmem()],
        out_specs=vmem(),
        out_shape=jax.ShapeDtypeStruct((64, 2 * HEAD), F32),
        compiler_params=params(VMEM_LITTLE),
    )(where, mine, other)


def place_kernel(where_ref, *refs):
    for k in range(XS):
        plane = (where_ref[0] - k) & 3
        for half in range(2):
            refs[XS][pl.ds(pl.multiple_of((half * 4 + plane) * 32, 32), 32), :] = refs[k][
                half * 32 : (half + 1) * 32
            ]


def place(where, shares):
    return pl.pallas_call(
        place_kernel,
        in_specs=[smem()] + [vmem()] * XS,
        out_specs=vmem(),
        out_shape=jax.ShapeDtypeStruct((SEG_LEN, 2 * HEAD), F32),
        compiler_params=params(VMEM_LITTLE),
    )(where, *shares)


def ancestors_of(parents_ref, seg):
    first = parents_ref[0, seg]
    second = parents_ref[0, first]
    third = parents_ref[0, second]
    return first, second, third


def select_kernel(parents_ref, owners_ref, in_ref, out_ref):
    def step(seg, carry):
        holder = owners_ref[0, seg]
        for k, ancestor in enumerate(ancestors_of(parents_ref, seg)):
            out_ref[holder, k] = in_ref[owners_ref[0, ancestor]]
        return carry

    lax.fori_loop(0, SEGS, step, 0)


def select_chunks(parents, owners, chunks):
    return pl.pallas_call(
        select_kernel,
        in_specs=[smem(), smem(), vmem()],
        out_specs=vmem(),
        out_shape=jax.ShapeDtypeStruct((SEGS, DEPTH - 1, CHUNK, HEAD), BF16),
        compiler_params=params(),
    )(parents, owners, chunks)


def collect_kernel(parents_ref, owners_ref, in_ref, out_ref):
    out_ref[...] = jnp.zeros_like(out_ref)

    def step(seg, carry):
        holder = owners_ref[0, seg]
        for k, ancestor in enumerate(ancestors_of(parents_ref, seg)):
            target = owners_ref[0, ancestor]
            out_ref[target] += in_ref[holder, k].astype(F32)
        return carry

    lax.fori_loop(0, SEGS, step, 0)


def collect_chunks(parents, owners, grads):
    return pl.pallas_call(
        collect_kernel,
        in_specs=[smem(), smem(), vmem()],
        out_specs=vmem(),
        out_shape=jax.ShapeDtypeStruct((SEGS, CHUNK, HEAD), F32),
        compiler_params=params(),
    )(parents, owners, grads)


def dot_nt(a, b):
    return lax.dot_general(a, b, (((1,), (1,)), ((), ())), preferred_element_type=F32)


def dot_nn(a, b):
    return jnp.dot(a, b, preferred_element_type=F32)


def attend_kernel(
    depth_ref, own_ref, anc_ref, q_ref, g_ref,
    out_ref, qgrad_ref, own_grad_ref, anc_grad_ref,
    keys_ref, values_ref, keys_t_ref, values_t_ref, dk_ref, dv_ref,
):
    step = pl.program_id(0)
    factor = HEAD ** (-0.5)
    log2_factor = factor * math.log2(math.e)
    half = SEGS // 2
    blocks = [slice(b * SEG_LEN, (b + 1) * SEG_LEN) for b in range(DEPTH)]

    @pl.when(step == 0)
    def _():
        keys_ref[blocks[0]] = own_ref[0:SEG_LEN]
        values_ref[blocks[0]] = own_ref[SEG_LEN : 2 * SEG_LEN]
        for b in range(1, DEPTH):
            keys_ref[blocks[b]] = anc_ref[0:half, b - 1].reshape(SEG_LEN, HEAD)
            values_ref[blocks[b]] = anc_ref[half:SEGS, b - 1].reshape(SEG_LEN, HEAD)
        keys_t_ref[...] = keys_ref[...].T
        values_t_ref[...] = values_ref[...].T
        dk_ref[...] = jnp.zeros_like(dk_ref)
        dv_ref[...] = jnp.zeros_like(dv_ref)

    depth = depth_ref[0]
    causal = lax.broadcasted_iota(jnp.int32, (SEG_LEN, SEG_LEN), 0) <= lax.broadcasted_iota(
        jnp.int32, (SEG_LEN, SEG_LEN), 1
    )
    for h in range(STEP_HEADS):
        cols = slice(h * HEAD, (h + 1) * HEAD)
        q = q_ref[:, cols]
        g = g_ref[:, cols]
        scores = []
        for b in range(DEPTH):
            block = dot_nt(keys_ref[blocks[b]], q)
            if b == 0:
                block = jnp.where(causal, block, -jnp.inf)
            else:
                block = block + jnp.where(depth >= b, 0.0, -jnp.inf)
            scores.append(block)
        peak = jnp.max(functools.reduce(jnp.maximum, scores), axis=0, keepdims=True) * log2_factor
        expd = [jnp.exp2(block * log2_factor - peak) for block in scores]
        scale = 1.0 / sum(jnp.sum(block, axis=0, keepdims=True) for block in expd)
        probs = [(block * scale).astype(BF16) for block in expd]
        dprobs = [dot_nt(values_ref[blocks[b]], g) for b in range(DEPTH)]
        centre = sum(
            jnp.sum(p.astype(F32) * dp, axis=0, keepdims=True) for p, dp in zip(probs, dprobs)
        )
        dscores = [(p.astype(F32) * (dp - centre)).astype(BF16) for p, dp in zip(probs, dprobs)]
        probs = jnp.concatenate(probs, axis=0)
        dscores = jnp.concatenate(dscores, axis=0)
        out_ref[:, cols] = dot_nn(values_t_ref[...], probs).T.astype(BF16)
        qgrad_ref[:, cols] = (dot_nn(keys_t_ref[...], dscores).T * factor).astype(BF16)
        dk_ref[...] += dot_nn(dscores, q)
        dv_ref[...] += dot_nn(probs, g)

    @pl.when(step == HEADS // STEP_HEADS - 1)
    def _():
        own_grad_ref[0:SEG_LEN] = dk_ref[blocks[0]] * factor
        own_grad_ref[SEG_LEN : 2 * SEG_LEN] = dv_ref[blocks[0]]
        for b in range(1, DEPTH):
            anc_grad_ref[0:half, b - 1] = (
                (dk_ref[blocks[b]] * factor).astype(BF16).reshape(half, CHUNK, HEAD)
            )
            anc_grad_ref[half:SEGS, b - 1] = (
                dv_ref[blocks[b]].astype(BF16).reshape(half, CHUNK, HEAD)
            )


def attend(depth, own, anc, queries, grads):
    head = pl.BlockSpec((SEG_LEN, STEP_HEADS * HEAD), lambda h: (0, h))
    keys = DEPTH * SEG_LEN
    return pl.pallas_call(
        attend_kernel,
        grid=(HEADS // STEP_HEADS,),
        in_specs=[
            smem(),
            pl.BlockSpec((2 * SEG_LEN, HEAD), lambda h: (0, 0)),
            pl.BlockSpec((SEGS, DEPTH - 1, CHUNK, HEAD), lambda h: (0, 0, 0, 0)),
            head,
            head,
        ],
        out_specs=[
            head,
            head,
            pl.BlockSpec((2 * SEG_LEN, HEAD), lambda h: (0, 0)),
            pl.BlockSpec((SEGS, DEPTH - 1, CHUNK, HEAD), lambda h: (0, 0, 0, 0)),
        ],
        out_shape=[
            jax.ShapeDtypeStruct((SEG_LEN, HEADS * HEAD), BF16),
            jax.ShapeDtypeStruct((SEG_LEN, HEADS * HEAD), BF16),
            jax.ShapeDtypeStruct((2 * SEG_LEN, HEAD), F32),
            jax.ShapeDtypeStruct((SEGS, DEPTH - 1, CHUNK, HEAD), BF16),
        ],
        scratch_shapes=[
            pltpu.VMEM((keys, HEAD), BF16),
            pltpu.VMEM((keys, HEAD), BF16),
            pltpu.VMEM((HEAD, keys), BF16),
            pltpu.VMEM((HEAD, keys), BF16),
            pltpu.VMEM((keys, HEAD), F32),
            pltpu.VMEM((keys, HEAD), F32),
        ],
        compiler_params=params(VMEM_MOST),
        cost_estimate=pl.CostEstimate(
            flops=0, bytes_accessed=0, transcendentals=0
        ),
    )(depth, own, anc, queries, grads)


def x_shift(value, steps, flip=0):
    pairs = [(i, ((i + 2 * steps) % LEAVES) ^ flip) for i in range(LEAVES)]
    return lax.ppermute(value, "leaf", pairs)


def core_swap(value):
    return x_shift(value, 0, 1)


def y_shift(value, steps):
    return lax.ppermute(value, "seg", [(i, (i + ZS * steps) % SEGS) for i in range(SEGS)])


def z_shift(value, steps):
    pairs = [(i, i // ZS * ZS + (i + steps) % ZS) for i in range(SEGS)]
    return lax.ppermute(value, "seg", pairs)


def over_z(value):
    groups = [list(range(i, i + ZS)) for i in range(0, SEGS, ZS)]
    return lax.all_to_all(value, "seg", 0, 0, axis_index_groups=groups, tiled=True)


def over_seg(value):
    return lax.all_to_all(value, "seg", 0, 0, tiled=True)


def per_device(hidden_states, queries, key_value_weight, attention_grad, parents, owners, depths):
    leaf = lax.axis_index("leaf")
    position = lax.axis_index("seg")
    x, core, y = leaf // 2, leaf % 2, position // ZS
    where = jnp.stack([x, core, y, position % ZS]).astype(jnp.int32)
    depth = jnp.sum(jnp.where(owners[0] == position, depths[0], 0)).reshape(1)

    tokens = hidden_states[0]
    half = lax.dynamic_slice_in_dim(key_value_weight, core * 128, 128, 0)
    theirs = core_swap(tokens)
    near = jnp.concatenate([half, y_shift(half, -1)])
    far = jnp.concatenate([y_shift(half, -2), y_shift(half, -3)])
    pieces = []
    for first, way in ((near, -1), (far, 1)):
        ring = {0: first}
        for d in range(1, 4):
            ring[d] = z_shift(ring[d - 1], -1)
            ring[8 - d] = z_shift(ring[(9 - d) % 8], 1)
        ring[4] = z_shift(ring[4 + way], way)
        pieces.extend(ring[d] for d in range(8))
    own_part, their_part = project(where, tokens, theirs, pieces)
    stacked = stack(own_part, core_swap(their_part))

    stacked, theirs = lax.optimization_barrier((stacked, theirs))
    both1, both3 = shuffle(tokens, theirs, where, (1, 3))
    chunks = over_seg(stacked.reshape(SEGS, CHUNK, HEAD))
    chunks, both1, both3, theirs = lax.optimization_barrier((chunks, both1, both3, theirs))
    moved1, moved3 = x_shift(both1, 1), x_shift(both3, 3)
    both0, both2 = shuffle(tokens, theirs, where, (0, 2))
    ancestors = over_seg(select_chunks(parents, owners, chunks))
    ancestors, both0, both2 = lax.optimization_barrier((ancestors, both0, both2))
    output, query_grad, own_grad, anc_grad = attend(
        depth, stacked, ancestors, queries[0], attention_grad[0]
    )
    anc_grad, moved1, moved3, both2 = lax.optimization_barrier((anc_grad, moved1, moved3, both2))
    moved2 = x_shift(both2, 2)
    arrived = over_seg(anc_grad)
    returned = over_seg(collect_chunks(parents, owners, arrived))
    returned, moved2 = lax.optimization_barrier((returned, moved2))
    diff = (own_grad + returned.reshape(2 * SEG_LEN, HEAD)).astype(BF16)

    diffs = [diff] + [x_shift(diff, k) for k in range(1, XS)]
    swapped = [core_swap(d) for d in diffs]
    pairs = [d for k in range(XS) for d in (diffs[k], swapped[k])]
    columns = (both0, moved1, moved2, moved3)
    blocks = {e: gradient(columns, pairs, e) for e in (2, 1, 3, 0)}
    summed = blocks[0]
    for e in (1, 3, 2):
        summed = summed + y_shift(blocks[e], e)
    factor = float(LEAVES * SEGS * SEG_LEN) ** (-0.5)
    share = jnp.sum(over_z(summed.reshape(ZS, 32, 2 * HEAD)), axis=0) * factor
    share = pair_up(where, share, core_swap(share))
    grad_block = place(where, [share] + [x_shift(share, k) for k in range(1, XS)])
    return (output[None], query_grad[None], grad_block)


def solution(mesh):
    placed = (
        P("leaf", "seg", None),
        P("leaf", "seg", None),
        P("seg", None),
        P("leaf", "seg", None),
        P("leaf", None),
        P("leaf", None),
        P("leaf", None),
    )
    return jax.shard_map(
        per_device,
        mesh=mesh,
        in_specs=placed,
        out_specs=(P("leaf", "seg", None), P("leaf", "seg", None), P("seg", None)),
        check_vma=False,
    )
```

```python
import functools
import math

import jax
import jax.numpy as jnp
from jax import lax
from jax.experimental import pallas as pl
from jax.experimental.pallas import tpu as pltpu
from jax.sharding import PartitionSpec as P

HEAD = 128
HEADS = 8
DEPTH = 4
SEGS = 32
SEG_LEN = 256
LEAVES = 8
D = 8192
XS = 4
ZS = 8
STEP_HEADS = 2
CHUNK = 2 * SEG_LEN // SEGS
PART = D // LEAVES
F32 = jnp.float32
BF16 = jnp.bfloat16
VMEM_LIMIT = 40 * 1024 * 1024
VMEM_MOST = 60 * 1024 * 1024
VMEM_LITTLE = 16 * 1024 * 1024


def smem():
    return pl.BlockSpec(memory_space=pltpu.SMEM)


def vmem():
    return pl.BlockSpec(memory_space=pltpu.VMEM)


def params(limit=VMEM_LIMIT):
    return pltpu.CompilerParams(vmem_limit_bytes=limit)


def shuffle_kernel(planes, where_ref, own_ref, theirs_ref, out0_ref, out1_ref, perm_ref):
    x, core, y = where_ref[0], where_ref[1], where_ref[2]
    count = own_ref.shape[0]

    @pl.when(pl.program_id(0) == 0)
    def _():
        rows = lax.broadcasted_iota(jnp.int32, (512, 256), 0)
        cols = lax.broadcasted_iota(jnp.int32, (512, 256), 1)
        k = jnp.where(cols < 128, planes[0], planes[1])
        s4, r = (cols >> 5) & 3, cols & 31
        source = (s4 << 7) + (((x + k) & 3) << 5) + r
        perm_ref[...] = jnp.where(rows == source, 1.0, 0.0).astype(BF16)

    def group(g, carry):
        lanes = pl.ds(pl.multiple_of((((g >> 1) - y) & 3) * 256 + (g & 1) * 128, 128), 128)
        tiles = [
            jnp.concatenate(
                [
                    ref[:, pl.ds(pl.multiple_of((4 * g + s4) * 256 + core * 128, 128), 128)]
                    for s4 in range(4)
                ],
                axis=1,
            )
            for ref in (own_ref, theirs_ref)
        ]
        moved = jnp.dot(
            jnp.concatenate(tiles, axis=0), perm_ref[...], preferred_element_type=F32
        ).astype(BF16)
        for n in range(2):
            out0_ref[n, :, lanes] = moved[n * count : (n + 1) * count, 0:128]
            out1_ref[n, :, lanes] = moved[n * count : (n + 1) * count, 128:256]
        return carry

    lax.fori_loop(0, 8, group, 0, unroll=4)


def shuffle(tokens, theirs, where, planes):
    step = SEG_LEN // 2
    raw = pl.BlockSpec((step, D), lambda i: (i, 0))
    out = pl.pallas_call(
        functools.partial(shuffle_kernel, planes),
        grid=(2,),
        in_specs=[smem(), raw, raw],
        out_specs=[pl.BlockSpec((2, step, PART), lambda i: (0, i, 0))] * 2,
        out_shape=[jax.ShapeDtypeStruct((2, SEG_LEN, PART), BF16)] * 2,
        scratch_shapes=[pltpu.VMEM((512, 256), BF16)],
        compiler_params=params(VMEM_MOST),
        cost_estimate=pl.CostEstimate(
            flops=2 * 2 * SEG_LEN * 512 * 256 * 8, bytes_accessed=10 << 20, transcendentals=0
        ),
    )(where, tokens, theirs)
    return [block.reshape(2 * SEG_LEN, PART) for block in out]


def project_kernel(where_ref, own_ref, theirs_ref, *refs):
    pieces, outs = refs[:16], refs[16:]
    core, y, z = where_ref[1], where_ref[2], where_ref[3]
    for rows_ref, out_ref in ((own_ref, outs[0]), (theirs_ref, outs[1])):
        total = 0.0
        for n, ref in enumerate(pieces):
            tiles = []
            for e in (2 * (n // 8), 2 * (n // 8) + 1):
                shard = ((y + e) & 3) * ZS + ((z + n % 8) & 7)
                start = pl.multiple_of(shard * 256 + core * 128, 128)
                tiles.append(rows_ref[:, pl.ds(start, 128)])
            total = total + dot_nn(jnp.concatenate(tiles, axis=1), ref[...])
        out_ref[...] = total


def project(where, tokens, theirs, pieces):
    shape = jax.ShapeDtypeStruct((SEG_LEN, 2 * HEAD), F32)
    return pl.pallas_call(
        project_kernel,
        in_specs=[smem()] + [vmem()] * 18,
        out_specs=[vmem()] * 2,
        out_shape=[shape] * 2,
        compiler_params=params(VMEM_LITTLE),
        cost_estimate=pl.CostEstimate(
            flops=2 * 2 * SEG_LEN * D // 2 * 2 * HEAD, bytes_accessed=7 << 20, transcendentals=0
        ),
    )(where, tokens, theirs, *pieces)


def stack_kernel(a_ref, b_ref, out_ref):
    total = (a_ref[...] + b_ref[...]).astype(BF16)
    out_ref[0:SEG_LEN] = total[:, :HEAD]
    out_ref[SEG_LEN : 2 * SEG_LEN] = total[:, HEAD:]


def stack(a, b):
    return pl.pallas_call(
        stack_kernel,
        in_specs=[vmem()] * 2,
        out_specs=vmem(),
        out_shape=jax.ShapeDtypeStruct((2 * SEG_LEN, HEAD), BF16),
        compiler_params=params(),
    )(a, b)


def gradient_kernel(*refs):
    columns, diffs, out_ref = refs[:4], refs[4:12], refs[12]
    total = 0.0
    for k in range(XS):
        for n in range(2):
            d_ref = diffs[2 * k + n]
            both = jnp.concatenate([d_ref[0:SEG_LEN], d_ref[SEG_LEN : 2 * SEG_LEN]], axis=1)
            total = total + dot_nn(both.T, columns[k][n * SEG_LEN : (n + 1) * SEG_LEN])
    out_ref[...] = total.T


def gradient(columns, diffs, block):
    return pl.pallas_call(
        gradient_kernel,
        grid=(1,),
        in_specs=[pl.BlockSpec((2 * SEG_LEN, SEG_LEN), lambda i: (0, block))] * XS
        + [pl.BlockSpec((2 * SEG_LEN, HEAD), lambda i: (0, 0))] * LEAVES,
        out_specs=pl.BlockSpec((SEG_LEN, 2 * HEAD), lambda i: (0, 0)),
        out_shape=jax.ShapeDtypeStruct((SEG_LEN, 2 * HEAD), F32),
        compiler_params=params(),
        cost_estimate=pl.CostEstimate(
            flops=2 * LEAVES * SEG_LEN * SEG_LEN * 2 * HEAD, bytes_accessed=3 << 20, transcendentals=0
        ),
    )(*columns, *diffs)


def pair_kernel(where_ref, mine_ref, other_ref, out_ref):
    core = where_ref[1]
    out_ref[pl.ds(pl.multiple_of(core * 32, 32), 32), :] = mine_ref[...]
    out_ref[pl.ds(pl.multiple_of((1 - core) * 32, 32), 32), :] = other_ref[...]


def pair_up(where, mine, other):
    return pl.pallas_call(
        pair_kernel,
        in_specs=[smem(), vmem(), vmem()],
        out_specs=vmem(),
        out_shape=jax.ShapeDtypeStruct((64, 2 * HEAD), F32),
        compiler_params=params(VMEM_LITTLE),
    )(where, mine, other)


def place_kernel(where_ref, *refs):
    for k in range(XS):
        plane = (where_ref[0] - k) & 3
        for half in range(2):
            refs[XS][pl.ds(pl.multiple_of((half * 4 + plane) * 32, 32), 32), :] = refs[k][
                half * 32 : (half + 1) * 32
            ]


def place(where, shares):
    return pl.pallas_call(
        place_kernel,
        in_specs=[smem()] + [vmem()] * XS,
        out_specs=vmem(),
        out_shape=jax.ShapeDtypeStruct((SEG_LEN, 2 * HEAD), F32),
        compiler_params=params(VMEM_LITTLE),
    )(where, *shares)


def ancestors_of(parents_ref, seg):
    first = parents_ref[0, seg]
    second = parents_ref[0, first]
    third = parents_ref[0, second]
    return first, second, third


def select_kernel(parents_ref, owners_ref, in_ref, out_ref):
    def step(seg, carry):
        holder = owners_ref[0, seg]
        for k, ancestor in enumerate(ancestors_of(parents_ref, seg)):
            out_ref[holder, k] = in_ref[owners_ref[0, ancestor]]
        return carry

    lax.fori_loop(0, SEGS, step, 0)


def select_chunks(parents, owners, chunks):
    return pl.pallas_call(
        select_kernel,
        in_specs=[smem(), smem(), vmem()],
        out_specs=vmem(),
        out_shape=jax.ShapeDtypeStruct((SEGS, DEPTH - 1, CHUNK, HEAD), BF16),
        compiler_params=params(),
    )(parents, owners, chunks)


def collect_kernel(parents_ref, owners_ref, in_ref, out_ref):
    out_ref[...] = jnp.zeros_like(out_ref)

    def step(seg, carry):
        holder = owners_ref[0, seg]
        for k, ancestor in enumerate(ancestors_of(parents_ref, seg)):
            target = owners_ref[0, ancestor]
            out_ref[target] += in_ref[holder, k].astype(F32)
        return carry

    lax.fori_loop(0, SEGS, step, 0)


def collect_chunks(parents, owners, grads):
    return pl.pallas_call(
        collect_kernel,
        in_specs=[smem(), smem(), vmem()],
        out_specs=vmem(),
        out_shape=jax.ShapeDtypeStruct((SEGS, CHUNK, HEAD), F32),
        compiler_params=params(),
    )(parents, owners, grads)


def dot_nt(a, b):
    return lax.dot_general(a, b, (((1,), (1,)), ((), ())), preferred_element_type=F32)


def dot_nn(a, b):
    return jnp.dot(a, b, preferred_element_type=F32)


def attend_kernel(
    depth_ref, own_ref, anc_ref, q_ref, g_ref,
    out_ref, qgrad_ref, own_grad_ref, anc_grad_ref,
    keys_ref, values_ref, keys_t_ref, values_t_ref, dk_ref, dv_ref,
):
    step = pl.program_id(0)
    factor = HEAD ** (-0.5)
    log2_factor = factor * math.log2(math.e)
    half = SEGS // 2
    blocks = [slice(b * SEG_LEN, (b + 1) * SEG_LEN) for b in range(DEPTH)]

    @pl.when(step == 0)
    def _():
        keys_ref[blocks[0]] = own_ref[0:SEG_LEN]
        values_ref[blocks[0]] = own_ref[SEG_LEN : 2 * SEG_LEN]
        for b in range(1, DEPTH):
            keys_ref[blocks[b]] = anc_ref[0:half, b - 1].reshape(SEG_LEN, HEAD)
            values_ref[blocks[b]] = anc_ref[half:SEGS, b - 1].reshape(SEG_LEN, HEAD)
        keys_t_ref[...] = keys_ref[...].T
        values_t_ref[...] = values_ref[...].T
        dk_ref[...] = jnp.zeros_like(dk_ref)
        dv_ref[...] = jnp.zeros_like(dv_ref)

    depth = depth_ref[0]
    causal = lax.broadcasted_iota(jnp.int32, (SEG_LEN, SEG_LEN), 0) <= lax.broadcasted_iota(
        jnp.int32, (SEG_LEN, SEG_LEN), 1
    )
    for h in range(STEP_HEADS):
        cols = slice(h * HEAD, (h + 1) * HEAD)
        q = q_ref[:, cols]
        g = g_ref[:, cols]
        scores = []
        for b in range(DEPTH):
            block = dot_nt(keys_ref[blocks[b]], q)
            if b == 0:
                block = jnp.where(causal, block, -jnp.inf)
            else:
                block = block + jnp.where(depth >= b, 0.0, -jnp.inf)
            scores.append(block)
        peak = jnp.max(functools.reduce(jnp.maximum, scores), axis=0, keepdims=True) * log2_factor
        expd = [jnp.exp2(block * log2_factor - peak) for block in scores]
        scale = 1.0 / sum(jnp.sum(block, axis=0, keepdims=True) for block in expd)
        probs = [(block * scale).astype(BF16) for block in expd]
        dprobs = [dot_nt(values_ref[blocks[b]], g) for b in range(DEPTH)]
        centre = sum(
            jnp.sum(p.astype(F32) * dp, axis=0, keepdims=True) for p, dp in zip(probs, dprobs)
        )
        dscores = [(p.astype(F32) * (dp - centre)).astype(BF16) for p, dp in zip(probs, dprobs)]
        probs = jnp.concatenate(probs, axis=0)
        dscores = jnp.concatenate(dscores, axis=0)
        out_ref[:, cols] = dot_nn(values_t_ref[...], probs).T.astype(BF16)
        qgrad_ref[:, cols] = (dot_nn(keys_t_ref[...], dscores).T * factor).astype(BF16)
        dk_ref[...] += dot_nn(dscores, q)
        dv_ref[...] += dot_nn(probs, g)

    @pl.when(step == HEADS // STEP_HEADS - 1)
    def _():
        own_grad_ref[0:SEG_LEN] = dk_ref[blocks[0]] * factor
        own_grad_ref[SEG_LEN : 2 * SEG_LEN] = dv_ref[blocks[0]]
        for b in range(1, DEPTH):
            anc_grad_ref[0:half, b - 1] = (
                (dk_ref[blocks[b]] * factor).astype(BF16).reshape(half, CHUNK, HEAD)
            )
            anc_grad_ref[half:SEGS, b - 1] = (
                dv_ref[blocks[b]].astype(BF16).reshape(half, CHUNK, HEAD)
            )


def attend(depth, own, anc, queries, grads):
    head = pl.BlockSpec((SEG_LEN, STEP_HEADS * HEAD), lambda h: (0, h))
    keys = DEPTH * SEG_LEN
    return pl.pallas_call(
        attend_kernel,
        grid=(HEADS // STEP_HEADS,),
        in_specs=[
            smem(),
            pl.BlockSpec((2 * SEG_LEN, HEAD), lambda h: (0, 0)),
            pl.BlockSpec((SEGS, DEPTH - 1, CHUNK, HEAD), lambda h: (0, 0, 0, 0)),
            head,
            head,
        ],
        out_specs=[
            head,
            head,
            pl.BlockSpec((2 * SEG_LEN, HEAD), lambda h: (0, 0)),
            pl.BlockSpec((SEGS, DEPTH - 1, CHUNK, HEAD), lambda h: (0, 0, 0, 0)),
        ],
        out_shape=[
            jax.ShapeDtypeStruct((SEG_LEN, HEADS * HEAD), BF16),
            jax.ShapeDtypeStruct((SEG_LEN, HEADS * HEAD), BF16),
            jax.ShapeDtypeStruct((2 * SEG_LEN, HEAD), F32),
            jax.ShapeDtypeStruct((SEGS, DEPTH - 1, CHUNK, HEAD), BF16),
        ],
        scratch_shapes=[
            pltpu.VMEM((keys, HEAD), BF16),
            pltpu.VMEM((keys, HEAD), BF16),
            pltpu.VMEM((HEAD, keys), BF16),
            pltpu.VMEM((HEAD, keys), BF16),
            pltpu.VMEM((keys, HEAD), F32),
            pltpu.VMEM((keys, HEAD), F32),
        ],
        compiler_params=params(VMEM_MOST),
        cost_estimate=pl.CostEstimate(
            flops=0, bytes_accessed=0, transcendentals=0
        ),
    )(depth, own, anc, queries, grads)


def x_shift(value, steps, flip=0):
    pairs = [(i, ((i + 2 * steps) % LEAVES) ^ flip) for i in range(LEAVES)]
    return lax.ppermute(value, "leaf", pairs)


def core_swap(value):
    return x_shift(value, 0, 1)


def y_shift(value, steps):
    return lax.ppermute(value, "seg", [(i, (i + ZS * steps) % SEGS) for i in range(SEGS)])


def z_shift(value, steps):
    pairs = [(i, i // ZS * ZS + (i + steps) % ZS) for i in range(SEGS)]
    return lax.ppermute(value, "seg", pairs)


def over_z(value):
    groups = [list(range(i, i + ZS)) for i in range(0, SEGS, ZS)]
    return lax.all_to_all(value, "seg", 0, 0, axis_index_groups=groups, tiled=True)


def over_seg(value):
    return lax.all_to_all(value, "seg", 0, 0, tiled=True)


def per_device(hidden_states, queries, key_value_weight, attention_grad, parents, owners, depths):
    leaf = lax.axis_index("leaf")
    position = lax.axis_index("seg")
    x, core, y = leaf // 2, leaf % 2, position // ZS
    where = jnp.stack([x, core, y, position % ZS]).astype(jnp.int32)
    depth = jnp.sum(jnp.where(owners[0] == position, depths[0], 0)).reshape(1)

    tokens = hidden_states[0]
    half = lax.dynamic_slice_in_dim(key_value_weight, core * 128, 128, 0)
    theirs = core_swap(tokens)
    near = jnp.concatenate([half, y_shift(half, -1)])
    far = jnp.concatenate([y_shift(half, -2), y_shift(half, -3)])
    pieces = []
    for first, way in ((near, -1), (far, 1)):
        ring = {0: first}
        for d in range(1, 4):
            ring[d] = z_shift(ring[d - 1], -1)
            ring[8 - d] = z_shift(ring[(9 - d) % 8], 1)
        ring[4] = z_shift(ring[4 + way], way)
        pieces.extend(ring[d] for d in range(8))
    own_part, their_part = project(where, tokens, theirs, pieces)
    stacked = stack(own_part, core_swap(their_part))

    stacked, theirs = lax.optimization_barrier((stacked, theirs))
    both1, both3 = shuffle(tokens, theirs, where, (1, 3))
    chunks = over_seg(stacked.reshape(SEGS, CHUNK, HEAD))
    chunks, both1, both3, theirs = lax.optimization_barrier((chunks, both1, both3, theirs))
    moved1, moved3 = x_shift(both1, 1), x_shift(both3, 3)
    both0, both2 = shuffle(tokens, theirs, where, (0, 2))
    ancestors = over_seg(select_chunks(parents, owners, chunks))
    ancestors, both0, both2 = lax.optimization_barrier((ancestors, both0, both2))
    output, query_grad, own_grad, anc_grad = attend(
        depth, stacked, ancestors, queries[0], attention_grad[0]
    )
    anc_grad, moved1, moved3, both2 = lax.optimization_barrier((anc_grad, moved1, moved3, both2))
    moved2 = x_shift(both2, 2)
    arrived = over_seg(anc_grad)
    returned = over_seg(collect_chunks(parents, owners, arrived))
    returned, moved2 = lax.optimization_barrier((returned, moved2))
    diff = (own_grad + returned.reshape(2 * SEG_LEN, HEAD)).astype(BF16)

    diffs = [diff] + [x_shift(diff, k) for k in range(1, XS)]
    swapped = [core_swap(d) for d in diffs]
    pairs = [d for k in range(XS) for d in (diffs[k], swapped[k])]
    columns = (both0, moved1, moved2, moved3)
    blocks = {e: gradient(columns, pairs, e) for e in (2, 1, 3, 0)}
    summed = blocks[0]
    for e in (1, 3, 2):
        summed = summed + y_shift(blocks[e], e)
    factor = float(LEAVES * SEGS * SEG_LEN) ** (-0.5)
    share = jnp.sum(over_z(summed.reshape(ZS, 32, 2 * HEAD)), axis=0) * factor
    share = pair_up(where, share, core_swap(share))
    grad_block = place(where, [share] + [x_shift(share, k) for k in range(1, XS)])
    return (output[None], query_grad[None], grad_block)


def solution(mesh):
    placed = (
        P("leaf", "seg", None),
        P("leaf", "seg", None),
        P("seg", None),
        P("leaf", "seg", None),
        P("leaf", None),
        P("leaf", None),
        P("leaf", None),
    )
    return jax.shard_map(
        per_device,
        mesh=mesh,
        in_specs=placed,
        out_specs=(P("leaf", "seg", None), P("leaf", "seg", None), P("seg", None)),
        check_vma=False,
    )
```
